256 devices in a mesh: index: 128 (over z, x_hi, y, core), rep: 2 (over x_lo).
Axes of the slice: x: 4 (x_hi: 2, x_lo: 2; x = x_hi * 2 + x_lo), y: 4, z: 8, core: 2. Of those that a mesh axis runs over, the one named last changes fastest.
Arguments:
- queries: bfloat16 [128, 2, 8, 16, 512], P('index', 'rep'), may hold values from -6 to 6
- database: bfloat16 [512, 8, 16, 512], P('index'), may hold values from -6 to 6
- db_frames: int32 [512], P('index'), may hold values from 1 to 8
- cand_shard: int32 [128, 2, 128, 1], P('index', 'rep'), may hold values from 0 to 127; in each aligned block of 128 rows (0 to 127, 128 to 255, ..., all dimensions but the last counted through in order) at most 2 rows name the same one
- cand_local: int32 [128, 2, 128], P('index', 'rep'), may hold values from 0 to 3
- conv_one: float32 [3, 3, 1, 32], replicated, may hold values from -2 to 2
- conv_two: float32 [3, 3, 32, 64], replicated, may hold values from -0.375 to 0.375
- conv_three: float32 [3, 3, 64, 128], replicated, may hold values from -0.25 to 0.25
- conv_out: float32 [128], replicated, may hold values from -0.5 to 0.5
Outputs:
- coarse: float32 [2, 128, 512], P('rep', None, 'index')
- refined: float32 [128, 2, 128], P('index', 'rep')
The draws below stay inside these ranges and needn't reach their ends.
Inputs may be any that keep to these rules, and one draw needn't show every extreme that they name: `cand_shard`: among the 128 candidates of one query no shard is named more than 2 times, and some query names one shard exactly 2 times; a few shards are named far more often than others.
All inputs are finite; a program needn't handle non-finite values.
Results may differ from the reference program's by a relative error of at most 0.0003.
Values may be sent and summed in bfloat16 or wider, within the bound.
A program may use at most 128 MiB of HBM per device.

```python
import math
import jax
import jax.numpy as jnp
import numpy as np
from jax import lax

WIDTH = 512
REGIONS = 16
FRAMES = 8
DB_DEV = 4
CANDS = 128
CH_ONE = 32
CH_TWO = 64
CH_THREE = 128
QUERY_ROWS = 128
SETS = 2
DB_VIDEOS = 512
SLOTS = 2
N_INDEX = 128


def touch_ends(array, own_key, low, top_value):
    dims = array.shape
    spot = [jax.random.randint(jax.random.fold_in(own_key, axis), (), 0, dims[axis]) for axis in range(len(dims))]
    array = array.at[tuple(spot)].set(low)
    longest = dims.index(max(dims))
    spot[longest] = (spot[longest] + 1) % dims[longest]
    return array.at[tuple(spot)].set(top_value)


def block_scale(key, extent, split, low, top_value):
    factor_of, own = 1.0, jax.random.fold_in(key, 6)
    for axis_at, blocks in split:
        steps = jnp.exp(jax.random.uniform(jax.random.fold_in(own, axis_at), (blocks,), jnp.float32, low / len(split), top_value / len(split)))
        factor_of = factor_of * jnp.repeat(steps, extent[axis_at] // blocks).reshape([-1 if axis == axis_at else 1 for axis in range(len(extent))])
    return factor_of


def routed_block(rng, own, number, rows, count, top, reach, skew):
    ranking = jax.random.permutation(rng, count)
    heavy_load, common = portions_of(count, rows * top, reach, skew, True), portions_of(count, rows * top, reach, skew, False)
    places = jnp.arange(count)

    def named(sizes, turn):
        used = int((sizes > 0).sum())
        fixed = max(1, used // 4)
        moved = fixed + (places - fixed + turn * (used - fixed)) % max(1, count - fixed)
        return jnp.zeros((count,), jnp.int32).at[ranking[jnp.where(places < fixed, places, moved)]].set(jnp.asarray(sizes, jnp.int32))

    sizes = jnp.where(number % 4 == 0, named(heavy_load, number // 4), named(common, number - number // 4 - 1))
    mixed = jax.random.permutation(jax.random.fold_in(own, 3), count)
    source_of, taker = mixed[0:count // 2 * 2:2], mixed[1:count // 2 * 2:2]
    margin = jnp.minimum(sizes[source_of] - 1, reach - sizes[taker]) // 2
    margin = jnp.where((source_of == ranking[0]) | (taker == ranking[0]) | (sizes[taker] == 0), 0, jnp.maximum(margin, 0))
    moved = jax.random.randint(jax.random.fold_in(own, 4), (count // 2,), 0, 1 << 20) % (margin + 1)
    sizes = sizes.at[source_of].add(-moved).at[taker].add(moved)
    items = jnp.searchsorted(jnp.cumsum(sizes), jnp.arange(rows * top), side="right").astype(jnp.int32)
    listing = items.reshape(top, rows).T
    listing = listing[jax.random.permutation(jax.random.fold_in(own, 1), rows)]
    turn = jax.random.randint(jax.random.fold_in(own, 2), (rows, 1), 0, top)
    return jnp.take_along_axis(listing, (jnp.arange(top)[None, :] + turn) % top, axis=1)


def portions_of(count, total, bound, skew, full):
    portions = [(1 << 20) // math.isqrt(rank ** skew) + 1 for rank in range(1, count + 1)]
    largest = bound if full else min(bound, max(-(-total // count), total * portions[0] // sum(portions)))
    least = 1 if total - largest >= count - 1 else 0
    counts, spare = [largest] + [least] * (count - 1), total - largest - least * (count - 1)
    while spare > 0:
        movable = [i for i in range(1, count) if counts[i] < largest] or [i for i in range(1, count) if counts[i] < bound]
        mass, left = sum([portions[i] for i in movable]), spare
        for i in movable:
            addition = min(bound - counts[i], max(1, left * portions[i] // mass), spare)
            counts[i] = counts[i] + addition
            spare = spare - addition
    return np.array(counts)


def noise(rng, shape, spread, reach, shards=(), dtype=jnp.bfloat16):
    values = jax.random.normal(rng, shape, jnp.float32) * spread
    if len(shards) > 0:
        values = block_scale(rng, shape, shards, -0.22, 0.18) * values
    return jnp.clip(values, min=-reach, max=reach).astype(dtype)


def setup_inputs(seed: int = 0) -> dict:
    key_list = jax.random.split(jax.random.key(seed), 10)
    queries = noise(key_list[0], (QUERY_ROWS, SETS, FRAMES, REGIONS, WIDTH), 1.0, 6.0, ((0, 128), (1, 2)))
    database = noise(key_list[1], (DB_VIDEOS, FRAMES, REGIONS, WIDTH), 1.0, 6.0, ((0, 128),))
    db_frames = touch_ends(jax.random.randint(key_list[2], (DB_VIDEOS,), 1, FRAMES + 1), jax.random.fold_in(key_list[2], 1), 1, FRAMES).astype(jnp.int32)
    cand_shard_keys = jax.random.split(jax.random.fold_in(key_list[3], 1), QUERY_ROWS * SETS * CANDS // CANDS)
    cand_shard_turns = jax.random.permutation(jax.random.fold_in(key_list[3], 3), QUERY_ROWS * SETS * CANDS // CANDS)
    cand_shard = jax.vmap(lambda own, number: routed_block(jax.random.fold_in(key_list[3], 2), own, number, CANDS, N_INDEX, 1, SLOTS, 2))(cand_shard_keys, cand_shard_turns).reshape((QUERY_ROWS, SETS, CANDS, 1))
    cand_local = touch_ends(jax.random.randint(key_list[4], (QUERY_ROWS, SETS, CANDS), 0, DB_DEV), jax.random.fold_in(key_list[4], 1), 0, DB_DEV - 1).astype(jnp.int32)
    conv_one = noise(key_list[5], (3, 3, 1, CH_ONE), 9 ** -0.5, 2.0, (), jnp.float32)
    conv_two = noise(key_list[6], (3, 3, CH_ONE, CH_TWO), (9 * CH_ONE) ** -0.5, 0.375, (), jnp.float32)
    conv_three = noise(key_list[7], (3, 3, CH_TWO, CH_THREE), (9 * CH_TWO) ** -0.5, 0.25, (), jnp.float32)
    conv_out = noise(key_list[8], (CH_THREE,), CH_THREE ** -0.5, 0.5, (), jnp.float32)
    return dict(queries=queries, database=database, db_frames=db_frames, cand_shard=cand_shard, cand_local=cand_local, conv_one=conv_one, conv_two=conv_two, conv_three=conv_three, conv_out=conv_out)


HIGH = lax.Precision.HIGHEST


def block_frame_maps(query_block, clips):
    block_count, frame_count, region_count, feature_width = query_block.shape
    clip_count = clips.shape[0]
    left_rows = query_block.reshape(block_count * frame_count * region_count, feature_width)
    right_rows = clips.reshape(clip_count * frame_count * region_count, feature_width)
    similar = jnp.dot(left_rows, right_rows.T, preferred_element_type=jnp.float32) * (feature_width ** -0.5)
    similar = similar.reshape(block_count, frame_count, region_count, clip_count, frame_count, region_count)
    region_best = jnp.max(similar, axis=5)
    frame_map = jnp.mean(region_best, axis=2)
    return jnp.transpose(frame_map, (0, 2, 1, 3))


def chamfer(frame_map, lengths):
    frame_count = frame_map.shape[-1]
    present = jnp.arange(frame_count)[None, None, :] < lengths[:, None, None]
    masked = jnp.where(present, frame_map, -jnp.inf)
    return jnp.mean(jnp.max(masked, axis=2), axis=1)


def convolve(inputs, kernel):
    return lax.conv_general_dilated(inputs, kernel, (1, 1), "SAME", dimension_numbers=("NHWC", "HWIO", "NHWC"), precision=HIGH)


def network_score(frame_map, lengths, conv_one, conv_two, conv_three, conv_out):
    frame_count = frame_map.shape[-1]
    present = jnp.arange(frame_count)[None, None, :] < lengths[:, None, None]
    inputs = jnp.where(present, frame_map, 0.0)[..., None]
    hidden = jax.nn.relu(convolve(inputs, conv_one))
    hidden = jax.nn.relu(convolve(hidden, conv_two))
    hidden = jax.nn.relu(convolve(hidden, conv_three))
    output_map = jnp.einsum("bfgc,c->bfg", hidden, conv_out, precision=HIGH)
    return chamfer(output_map, lengths)


def reference(queries, database, db_frames, cand_shard, cand_local, conv_one, conv_two, conv_three, conv_out):
    flat_queries = queries.reshape((QUERY_ROWS * SETS,) + queries.shape[2:])
    cand_ids = (cand_shard[..., 0] * DB_DEV + cand_local).astype(jnp.int32).reshape(QUERY_ROWS * SETS, CANDS)

    def one_query(pair):
        query_video, chosen = pair
        frame_map = block_frame_maps(query_video[None], database)[0]
        coarse_row = chamfer(frame_map, db_frames)
        picked = jnp.take(frame_map, chosen, axis=0)
        picked_lengths = jnp.take(db_frames, chosen, axis=0)
        refined_row = network_score(picked, picked_lengths, conv_one, conv_two, conv_three, conv_out)
        return coarse_row, refined_row

    coarse_rows, refined_rows = lax.map(one_query, (flat_queries, cand_ids))
    coarse = jnp.transpose(coarse_rows.reshape(QUERY_ROWS, SETS, DB_VIDEOS), (1, 0, 2))
    refined = refined_rows.reshape(QUERY_ROWS, SETS, CANDS)
    return coarse, refined
```

```python
import functools

import jax
import jax.numpy as jnp
from jax import lax
from jax.experimental import pallas as pl
from jax.experimental.pallas import tpu as pltpu
from jax.sharding import PartitionSpec as P

MESH = pl.DeviceIdType.MESH
F32, BF16 = jnp.float32, jnp.bfloat16
ABSENT = -(2.0 ** 100)
K = 512


def dot(a, b):
    return jnp.dot(a, b, preferred_element_type=F32)


def iota(shape, axis):
    return lax.broadcasted_iota(jnp.int32, shape, axis)


def halves(x):
    high = x.astype(BF16)
    return high, (x - high.astype(F32)).astype(BF16)


def thirds(x):
    high, rest = x.astype(BF16), None
    rest = x - high.astype(F32)
    mid = rest.astype(BF16)
    return high, mid, (rest - mid.astype(F32)).astype(BF16)


def pick(onehot, x):
    y = dot(onehot, jnp.concatenate(thirds(x), axis=1))
    n = x.shape[1]
    return y[:, :n] + (y[:, n:2 * n] + y[:, 2 * n:])


def kernel(
    q_hbm, db_hbm, frames, shard_hbm, local_hbm, one_hbm, two_hbm, three_hbm, out_hbm,
    coarse_ref, refined_ref,
    qbuf, dbraw, dbp, fmap, lens, msg, rbuf, cbuf, perm, fold,
    shard_v, local_v, one_v, two_v, three_v, out_v,
    w1, w2, w3h, w3l, x1, x2h, x2l, pen, best,
    send_sem, recv_sem, msg_send, msg_recv, local_sem,
):
    index, rep = lax.axis_index("index"), lax.axis_index("rep")
    c, y, xh, z = index % 2, (index // 2) % 4, (index // 8) % 2, index // 16
    x = xh * 2 + rep
    a, b = y // 2, ((y + 1) // 2) % 2
    ell = rep

    def device(z, x, y, c):
        return (((z * 2 + x // 2) * 4 + y) * 2 + c, x % 2)

    def y_of(a, b):
        return a * 3 + b * (1 - 2 * a)

    me_q = z * 4 + a * 2 + c
    me_b = xh * 2 + b
    b_own, b_q, b_r, b_s = me_b, (1 - xh) * 2 + b, xh * 2 + (1 - b), (1 - xh) * 2 + (1 - b)
    dev = {
        "+": device((z + 1) % 8, x, y, c),
        "-": device((z + 7) % 8, x, y, c),
        "a": device(z, x, 3 - y, c),
        "b": device(z, x, y_of(a, 1 - b), c),
        "d": device(z, x, y, 1 - c),
        "xh": device(z, 3 - x, y, c),
        "xl": device(z, xh * 2 + (1 - rep), y, c),
        "c1": device(z, (1 - xh) * 2 + rep, y, c),
        "c3": device(z, (1 - xh) * 2 + rep, y_of(a, 1 - b), c),
    }

    def row_device(k, da, dc):
        off = ((k + 1) // 2) * (1 - 2 * (k % 2))
        zk, ak, ck = (z + off + 8) % 8, (a + da) % 2, (c + dc) % 2
        return zk, ak, ck, device(zk, x, y_of(ak, b), ck)

    barrier = pltpu.get_barrier_semaphore()

    def greet(t, _):
        pl.semaphore_signal(
            barrier, inc=1, device_id=row_device(t // 4, (t // 2) % 2, t % 2)[3], device_id_type=MESH
        )
        return 0

    lax.fori_loop(1, 32, greet, 0)
    for name in ("b", "c1", "c3", "xh", "xl"):
        pl.semaphore_signal(barrier, inc=1, device_id=dev[name], device_id_type=MESH)

    loads = [
        pltpu.make_async_copy(src, dst, local_sem.at[i])
        for i, (src, dst) in enumerate((
            (q_hbm, qbuf.at[me_q]),
            (db_hbm, dbraw.at[pl.ds(me_b * 4, 4)]),
            (three_hbm, three_v),
            (two_hbm, two_v),
            (one_hbm, one_v),
            (shard_hbm, shard_v),
            (local_hbm, local_v),
            (out_hbm, out_v),
        ))
    ]
    for load in loads:
        load.start()

    row8 = iota((8, 128), 0)
    for h in range(2):
        lens[me_b, pl.ds(h * 8, 8), :] = jnp.where(
            row8 % 2 == 0, frames[h * 2].astype(F32), frames[h * 2 + 1].astype(F32)
        )

    ids, started = {}, []

    def copy(name, src, dst, target):
        sem = ids.setdefault(name, len(ids))
        return pltpu.make_async_remote_copy(
            src_ref=src, dst_ref=dst, send_sem=send_sem.at[sem], recv_sem=recv_sem.at[sem],
            device_id=target, device_id_type=MESH,
        )

    def send(name, src, dst, target):
        started.append(copy(name, src, dst, target))
        started[-1].start()

    def wait(name, dst):
        copy(name, dst, dst, dev["d"]).wait_recv()

    def z_at(k):
        return (z + ((k + 1) // 2) * (1 - 2 * (k % 2)) + 8) % 8

    def half(zz, aa, h):
        return qbuf.at[zz * 4 + aa * 2 + c, pl.ds(h * 64, 64), :]

    def unit(zz, aa, cc):
        return qbuf.at[zz * 4 + aa * 2 + cc]

    def db_unit(block, u):
        return dbraw.at[block * 4 + u]

    pl.semaphore_wait(barrier, 36)

    def ring_send(way, d, item):
        k = 2 * (d - 1) - (1 if way == "+" else 0) if d > 1 else 0
        zz = z_at(k)
        ref = half(zz, 1 - a, 0) if item == 2 else half(zz, a, item)
        src = q_hbm.at[pl.ds(item * 64, 64), :] if d == 1 and item < 2 else ref
        send((way, d, item), src, ref, dev[way])

    def ring_wait(way, d, item):
        zz = z_at(2 * d - (1 if way == "+" else 0))
        wait((way, d, item), half(zz, 1 - a, 0) if item == 2 else half(zz, a, item))

    for h in range(2):
        ring_send("+", 1, h)
        ring_send("-", 1, h)
        send(("a", 0, h), q_hbm.at[pl.ds(h * 64, 64), :], half(z, a, h), dev["a"])

    def db_send(link, position):
        u = (2 * (1 - ell) + 1 + (3 * (position % 2)) + 2 * (position // 2)) % 4 if link == "xh" else (
            2 * (1 - ell) + position) % 4
        send((link, position), db_hbm.at[u], db_unit(me_b, u), dev[link])

    def db_wait(link, position):
        u = (2 * ell + 1 + (3 * (position % 2)) + 2 * (position // 2)) % 4 if link == "xh" else (
            2 * (1 - ell) + position) % 4
        wait((link, position), db_unit(b_q if link == "xh" else b_r, u))

    for position in range(2):
        db_send("xh", position)
        db_send("b", position)
    send(("d", 0, 0), q_hbm, unit(z, a, c), dev["d"])
    for name in ("b", "c1", "c3"):
        send(("len", name), lens.at[me_b], lens.at[me_b], dev[name])

    ri, ci = iota((256, 256), 0), iota((256, 256), 1)
    perm[...] = jnp.where(
        ci == (ri % 2) * 128 + ((ri // 2) % 8) * 16 + ri // 16, 1.0, 0.0
    ).astype(BF16)
    ri, ci = iota((256, 128), 0), iota((256, 128), 1)
    fold[...] = jnp.where((ri % 128) // 16 == ci // 16, 1.0 / 16.0, 0.0).astype(BF16)

    def permute(block, h):
        raw = dbraw[pl.ds(block * 4 + h * 2, 2)].reshape(256, K)
        dbp[block * 2 + h] = dot(perm[...], raw).astype(BF16)

    hbs = [
        b_own * 2, b_own * 2 + 1, b_q * 2 + ell, b_r * 2 + (1 - ell), b_s * 2 + ell,
        b_q * 2 + (1 - ell), b_r * 2 + ell, b_s * 2 + (1 - ell),
    ]

    def hb_at(o):
        total = jnp.int32(0)
        for i, value in enumerate(hbs):
            total = total + jnp.where(o == i, value, 0)
        return total

    def tile(hb, zz):
        left = dbp[hb]
        for n in range(2):
            right = qbuf[pl.ds(zz * 4 + n * 2, 2)].reshape(256, K)
            sim = lax.dot_general(left, right, (((1,), (1,)), ((), ())), preferred_element_type=F32)
            top = sim[0:16]
            for u in range(1, 16):
                top = jnp.maximum(top, sim[u * 16:(u + 1) * 16])
            for i in range(2):
                fmap[zz * 4 + n * 2 + i, hb] = top[:, i * 128:(i + 1) * 128]

    def tiles(os, ks):
        no, nk = len(os), len(ks)

        def body(t, _):
            tile(hb_at(os[0] + t % no), z_at(ks[0] + t // no))
            return 0

        lax.fori_loop(0, no * nk, body, 0)

    lane = iota((8, 128), 1)
    lane16 = lane % 16

    def post(k, first):
        zz = z_at(k)
        big = fmap[pl.ds(zz * 4, 4)].reshape(512, 128)
        maps = dot(jnp.concatenate(halves(big), axis=1), fold[...]) * (K ** -0.5)
        rows = jnp.zeros((8, 128), F32)
        for i in range(4):
            message = jnp.zeros((8, 128), F32)
            summit = jnp.zeros((8, 128), F32)
            for hb in range(8):
                length = lens[hb // 2, pl.ds((hb % 2) * 8, 8), :]
                parts = []
                for gh in range(2):
                    at = i * 128 + hb * 16 + gh * 8
                    present = (gh * 4 + row8 // 2).astype(F32) < length
                    parts.append(jnp.where(present, maps[at:at + 8], ABSENT))
                    message = jnp.where(lane16 == hb * 2 + gh, parts[-1], message)
                summit = jnp.where(lane16 // 2 == hb, jnp.maximum(*parts), summit)
            msg[zz * 4 + i] = message
            summit = jnp.maximum(summit, pltpu.roll(summit, 4, 0))
            summit = jnp.maximum(summit, pltpu.roll(summit, 2, 0))
            summit = jnp.where((row8 == lane % 2) & (row8 < 2), summit, 0.0)
            rows = jnp.where(row8 == i, jnp.sum(summit, axis=0, keepdims=True), rows)
        cbuf[me_b, zz] = rows
        for da in range(2):
            for dc in range(2):
                zk, ak, ck, target = row_device(k, da, dc)
                slot = zk * 4 + ak * 2 + ck
                if first and da == 0 and dc == 0:
                    rbuf[me_q] = msg[slot]
                else:
                    sem = k * 4 + da * 2 + dc
                    pltpu.make_async_remote_copy(
                        src_ref=msg.at[slot], dst_ref=rbuf.at[me_q], send_sem=msg_send.at[sem],
                        recv_sem=msg_recv.at[sem], device_id=target, device_id_type=MESH,
                    ).start()

    def weights_three():
        loads[2].wait()
        zero = jnp.zeros((64, 128), F32)
        for i in range(3):
            w = [three_v[(i * 3 + j) * 64:(i * 3 + j + 1) * 64, :] for j in range(3)]
            for r, (left, right) in enumerate(((w[1], w[0]), (w[2], w[1]), (zero, w[2]), (w[0], zero))):
                for s, part in enumerate((left, right)):
                    high, low = halves(part)
                    w3h[i, r * 64:(r + 1) * 64, s * 128:(s + 1) * 128] = high
                    w3l[i, r * 64:(r + 1) * 64, s * 128:(s + 1) * 128] = low

    def weights_rest():
        loads[3].wait()
        loads[4].wait()
        place = [jnp.where(iota((64, 128), 1) == iota((64, 128), 0) + 64 * s, 1.0, 0.0).astype(BF16) for s in range(2)]
        zero = jnp.zeros((32, 64), F32)
        for i in range(3):
            w = [two_v[(i * 3 + j) * 32:(i * 3 + j + 1) * 32, :] for j in range(3)]
            stacks = (jnp.concatenate(w + [zero], axis=0), jnp.concatenate([zero] + w, axis=0))
            for part in range(2):
                value = sum(dot(halves(stack)[part], where) for stack, where in zip(stacks, place)).astype(BF16)
                for r in range(2):
                    w2[i, r * 128:(r + 1) * 128, part * 128:(part + 1) * 128] = value
        spread = jnp.where(iota((32, 512), 1) % 32 == iota((32, 512), 0), 1.0, 0.0).astype(BF16)
        w1[...] = jnp.zeros((256, 512), BF16)
        j, col = iota((16, 512), 0), iota((16, 512), 1)
        g = (j % 2) * 4 + (j % 8) // 2
        pos = 2 * (col // 128) - 1 + (col % 128) // 32
        for part in range(2):
            for i in range(3):
                value = jnp.zeros((16, 512), F32)
                for s in range(3):
                    line = jnp.broadcast_to(one_v[i * 3 + s:i * 3 + s + 1, :], (16, 32))
                    line = dot(halves(line)[part], spread)
                    hit = (g - pos + 1 == s) & (pos >= 0) & (pos < 8)
                    value = value + jnp.where(hit, line, 0.0)
                w1[part * 128 + i * 16:part * 128 + (i + 1) * 16, :] = value.astype(BF16)

    def clear():
        none = jnp.zeros((128, 256), BF16)
        for p in range(4):
            x1[p, 0] = none
            x1[p, 9] = none
        for p in range(6):
            x2h[p, 0] = none
            x2h[p, 9] = none
            x2l[p, 0] = none
            x2l[p, 9] = none

        def edge(f, _):
            side = jnp.zeros((128, 128), BF16)
            x2h[1, f, :, 128:256] = side
            x2l[1, f, :, 128:256] = side
            x2h[4, f, :, 128:256] = side
            x2l[4, f, :, 128:256] = side
            return 0

        lax.fori_loop(1, 9, edge, 0)

    def share(way, d):
        k = 2 * d - (1 if way == "+" else 0)
        zz = z_at(k)
        send(("a", k, 1), half(zz, a, 1), half(zz, a, 1), dev["a"])
        send(("d", k, 0), unit(zz, a, c), unit(zz, a, c), dev["d"])

    def share_other(k):
        zz = z_at(k)
        send(("d", k, 1), unit(zz, 1 - a, c), unit(zz, 1 - a, c), dev["d"])

    def slab_wait(k):
        zz = z_at(k)
        wait(("d", k, 0), unit(zz, a, 1 - c))
        wait(("d", k, 1), unit(zz, 1 - a, 1 - c))

    def main_items(d):
        for item in range(2):
            for way in "+-":
                if d == 4 and way == "-":
                    continue
                ring_wait(way, d, item)
                if d < 3 or (d == 3 and way == "+"):
                    ring_send(way, d + 1, item)
        for way in "+-":
            if d < 4 or way == "+":
                share(way, d)

    def other_items(d):
        for way in "+-":
            if d == 4 and way == "+":
                continue
            ring_wait(way, d, 2)
            if d < 3 or (d == 3 and way == "-"):
                ring_send(way, d + 1, 2)
        for k in (2 * d - 1, 2 * d):
            if k < 8:
                wait(("a", k, 1), half(z_at(k), 1 - a, 1))
                share_other(k)

    loads[0].wait()
    wait(("a", 0, 0), half(z, 1 - a, 0))
    for way in "+-":
        ring_send(way, 1, 2)
    weights_three()
    wait(("a", 0, 1), half(z, 1 - a, 1))
    share_other(0)
    loads[1].wait()
    permute(b_own, 0)
    permute(b_own, 1)
    main_items(1)
    db_wait("xh", 0)
    send(("b", 4), db_unit(b_q, 2 * ell + 1), db_unit(b_q, 2 * ell + 1), dev["b"])
    db_wait("b", 0)
    send(("xh", 4), db_unit(b_r, 2 * (1 - ell)), db_unit(b_r, 2 * (1 - ell)), dev["xh"])
    for position in range(2, 4):
        db_send("xh", position)
        db_send("b", position)
    slab_wait(0)
    tiles((0, 1), (0,))
    weights_rest()
    other_items(1)
    clear()
    db_wait("xh", 1)
    db_wait("b", 1)
    permute(b_q, ell)
    permute(b_r, 1 - ell)
    slab_wait(1)
    slab_wait(2)
    tiles((0, 1, 2, 3), (1,))
    main_items(2)
    wait(("b", 4), db_unit(b_s, 2 * ell + 1))
    send(("xl", 1), db_unit(b_s, 2 * ell + 1), db_unit(b_s, 2 * ell + 1), dev["xl"])
    wait(("xh", 4), db_unit(b_s, 2 * ell))
    send(("xl", 0), db_unit(b_s, 2 * ell), db_unit(b_s, 2 * ell), dev["xl"])
    permute(b_s, ell)
    tiles((0, 1, 2, 3), (2,))
    other_items(2)
    tiles((2, 3), (0,))
    main_items(3)
    tiles((4,), (0, 1, 2))
    slab_wait(3)
    slab_wait(4)
    tiles((0, 1, 2, 3, 4), (3,))
    other_items(3)
    tiles((0, 1, 2, 3, 4), (4,))
    for position in range(2, 4):
        db_wait("xh", position)
        db_wait("b", position)
    permute(b_q, 1 - ell)
    permute(b_r, ell)
    main_items(4)
    tiles((5, 6), (0, 1, 2, 3, 4))
    other_items(4)
    for i in range(2):
        wait(("xl", i), db_unit(b_s, 2 * (1 - ell) + i))
    permute(b_s, 1 - ell)
    tiles((7,), (0, 1, 2, 3, 4))
    for name, block in (("b", b_r), ("c1", b_q), ("c3", b_s)):
        wait(("len", name), lens.at[block])
    post(0, True)

    def post_loop(k, _):
        post(k, False)
        return 0

    lax.fori_loop(1, 5, post_loop, 0)
    slab_wait(5)
    slab_wait(6)
    tiles((0, 1, 2, 3, 4, 5, 6, 7), (5, 6))
    slab_wait(7)
    tiles((0, 1, 2, 3, 4, 5, 6, 7), (7,))
    lax.fori_loop(5, 8, post_loop, 0)
    for name in ("b", "c1", "c3"):
        send(("coarse", name), cbuf.at[me_b], cbuf.at[me_b], dev[name])

    def column(row):
        return jnp.sum(
            jnp.where(iota((128, 128), 0) == iota((128, 128), 1), row.astype(F32), 0.0), axis=1, keepdims=True
        ).astype(jnp.int32)

    for i in (5, 6, 7):
        loads[i].wait()
    shard, place = column(shard_v[...]), column(local_v[...])
    cy = (shard // 2) % 4
    ca, cb = cy // 2, ((cy + 1) // 2) % 2
    source = (shard // 16) * 4 + ca * 2 + shard % 2
    chb = (((shard // 8) % 2) * 2 + cb) * 2 + place // 2
    base = source * 8 + place % 2
    cols = iota((128, 256), 1)
    onehot = jnp.concatenate(
        [jnp.where(cols == base + gl * 2, 1.0, 0.0).astype(BF16) for gl in range(4)], axis=0
    )

    def msg_copy(k, da, dc):
        off = ((k + 1) // 2) * (1 - 2 * (k % 2))
        slot = ((z - off + 8) % 8) * 4 + ((a + da) % 2) * 2 + (c + dc) % 2
        sem = k * 4 + da * 2 + dc
        return pltpu.make_async_remote_copy(
            src_ref=msg.at[slot], dst_ref=rbuf.at[slot], send_sem=msg_send.at[sem],
            recv_sem=msg_recv.at[sem], device_id=dev["d"], device_id_type=MESH,
        )

    def msg_wait(t, _):
        msg_copy(t // 4, (t // 2) % 2, t % 2).wait_recv()
        return 0

    lax.fori_loop(1, 32, msg_wait, 0)
    chosen = pick(onehot, rbuf[...].reshape(256, 128))
    lane = iota((128, 128), 1)
    lane16 = lane % 16
    maps = jnp.zeros((128, 128), F32)
    for gl in range(4):
        t = chosen[gl * 128:(gl + 1) * 128]
        for bit in (4, 2, 1):
            t = jnp.where((chb // bit) % 2 == 1, pltpu.roll(t, 128 - 2 * bit, 1), t)
        if gl:
            t = pltpu.roll(t, 2 * gl, 1)
        maps = jnp.where(lane16 // 2 == gl, t, maps)
    there = maps > ABSENT / 2
    for g in range(8):
        at = (g % 4) * 2 + g // 4
        pen[g] = jnp.where(there, 0.0, -3e38)[:, at:at + 1]
    maps = jnp.where(there & (lane16 < 8), maps, 0.0)
    high = maps.astype(BF16).astype(F32)
    both = jnp.where(lane16 < 8, high, pltpu.roll(maps - high, 8, 1))
    for f in range(8):
        around = pltpu.roll(both, (128 - 16 * (f - 1)) % 128, 1) if f != 1 else both
        if f == 0:
            around = jnp.where(lane < 16, 0.0, around)
        if f == 7:
            around = jnp.where(lane // 16 == 2, 0.0, around)
        around = around.astype(BF16)
        out = jnp.maximum(dot(jnp.concatenate([around, around], axis=1), w1[...]), 0.0)
        high1, low1 = halves(out)
        for p in range(4):
            x1[p, f + 1, :, 0:128] = high1[:, p * 128:(p + 1) * 128]
            x1[p, f + 1, :, 128:256] = low1[:, p * 128:(p + 1) * 128]

    def second(p, _):
        out = jnp.zeros((1024, 256), F32)
        for i in range(3):
            out = out + dot(x1[p, i:i + 8].reshape(1024, 256), w2[i])
        out = jnp.maximum(out[:, :128] + out[:, 128:], 0.0)
        for ref, part in zip((x2h, x2l), halves(out)):
            part = part.reshape(8, 128, 128)
            ref[p + 1, 1:9, :, 0:128] = part
            ref[p, 1:9, :, 128:192] = part[:, :, 0:64]
            ref[p + 2, 1:9, :, 192:256] = part[:, :, 64:128]
        return 0

    lax.fori_loop(0, 4, second, 0)
    scale = jnp.concatenate([out_v[...], out_v[...]], axis=1)
    best[...] = jnp.full((1024, 1), -3e38, F32)

    def third(p, _):
        out = jnp.zeros((1024, 256), F32)
        for i in range(3):
            upper = x2h[p + 1, i:i + 8].reshape(1024, 256)
            lower = x2l[p + 1, i:i + 8].reshape(1024, 256)
            out = out + dot(upper, w3h[i]) + dot(lower, w3h[i]) + dot(upper, w3l[i])
        out = jnp.maximum(out, 0.0) * scale
        for s in range(2):
            total = jnp.sum(out[:, s * 128:(s + 1) * 128], axis=1, keepdims=True)
            total = total.reshape(8, 128, 1) + pen[2 * p + s][None]
            best[...] = jnp.maximum(best[...], total.reshape(1024, 1))
        return 0

    lax.fori_loop(0, 4, third, 0)
    mean = jnp.sum(best[...].reshape(8, 128, 1), axis=0) * 0.125
    refined_ref[...] = jnp.sum(
        jnp.where(iota((128, 128), 0) == iota((128, 128), 1), mean, 0.0), axis=0, keepdims=True
    )

    for name, block in (("b", b_r), ("c1", b_q), ("c3", b_s)):
        wait(("coarse", name), cbuf.at[block])
    n, col = iota((128, 256), 0), iota((128, 256), 1)
    ny = (n // 2) % 4
    want = (((n // 8) % 2) * 2 + ((ny + 1) // 2) % 2) * 64 + (n // 16) * 8 + (ny // 2) * 2 + n % 2
    scores = pick(jnp.where(col == want, 1.0, 0.0).astype(BF16), cbuf[...].reshape(256, 128))
    for shift in (64, 32, 16):
        scores = scores + pltpu.roll(scores, shift, 1)
    scores = scores * 0.125
    mine = scores
    for block in range(1, 4):
        mine = jnp.where(me_b == block, pltpu.roll(scores, 128 - 4 * block, 1), mine)
    coarse_ref[...] = mine[:, 0:4]

    for sent in started:
        sent.wait_send()

    def sent_wait(t, _):
        msg_copy(t // 4, (t // 2) % 2, t % 2).wait_send()
        return 0

    lax.fori_loop(1, 32, sent_wait, 0)


def local(queries, database, db_frames, cand_shard, cand_local, conv_one, conv_two, conv_three, conv_out):
    anywhere = pl.BlockSpec(memory_space=pl.ANY)
    vmem = pl.BlockSpec(memory_space=pltpu.VMEM)
    smem = pl.BlockSpec(memory_space=pltpu.SMEM)
    coarse, refined = pl.pallas_call(
        kernel,
        out_shape=(jax.ShapeDtypeStruct((128, 4), F32), jax.ShapeDtypeStruct((1, 128), F32)),
        in_specs=[anywhere, anywhere, smem] + [anywhere] * 6,
        out_specs=(vmem, vmem),
        scratch_shapes=[
            pltpu.VMEM((32, 128, K), BF16),
            pltpu.VMEM((16, 128, K), BF16),
            pltpu.VMEM((8, 256, K), BF16),
            pltpu.VMEM((32, 8, 16, 128), F32),
            pltpu.VMEM((4, 16, 128), F32),
            pltpu.VMEM((32, 8, 128), F32),
            pltpu.VMEM((32, 8, 128), F32),
            pltpu.VMEM((4, 8, 8, 128), F32),
            pltpu.VMEM((256, 256), BF16),
            pltpu.VMEM((256, 128), BF16),
            pltpu.VMEM((1, 128), jnp.int32),
            pltpu.VMEM((1, 128), jnp.int32),
            pltpu.VMEM((9, 32), F32),
            pltpu.VMEM((288, 64), F32),
            pltpu.VMEM((576, 128), F32),
            pltpu.VMEM((1, 128), F32),
            pltpu.VMEM((256, 512), BF16),
            pltpu.VMEM((3, 256, 256), BF16),
            pltpu.VMEM((3, 256, 256), BF16),
            pltpu.VMEM((3, 256, 256), BF16),
            pltpu.VMEM((4, 10, 128, 256), BF16),
            pltpu.VMEM((6, 10, 128, 256), BF16),
            pltpu.VMEM((6, 10, 128, 256), BF16),
            pltpu.VMEM((8, 128, 1), F32),
            pltpu.VMEM((1024, 1), F32),
            pltpu.SemaphoreType.DMA((72,)),
            pltpu.SemaphoreType.DMA((72,)),
            pltpu.SemaphoreType.DMA((32,)),
            pltpu.SemaphoreType.DMA((32,)),
            pltpu.SemaphoreType.DMA((8,)),
        ],
        compiler_params=pltpu.CompilerParams(
            collective_id=0, has_side_effects=True, vmem_limit_bytes=52 * 1024 * 1024
        ),
        cost_estimate=pl.CostEstimate(flops=13_000_000_000, bytes_accessed=2_000_000, transcendentals=0),
    )(
        queries.reshape(128, K), database.reshape(4, 128, K), db_frames, cand_shard.reshape(1, 128),
        cand_local.reshape(1, 128), conv_one.reshape(9, 32), conv_two.reshape(288, 64),
        conv_three.reshape(576, 128), conv_out.reshape(1, 128),
    )
    return coarse[None], refined[None]


def solution(mesh):
    in_specs = (
        P("index", "rep", None, None, None),
        P("index", None, None, None),
        P("index"),
        P("index", "rep", None, None),
        P("index", "rep", None),
        P(),
        P(),
        P(),
        P(),
    )
    out_specs = (P("rep", None, "index"), P("index", "rep", None))
    return jax.shard_map(local, mesh=mesh, in_specs=in_specs, out_specs=out_specs, check_vma=False)
```

```python
import functools

import jax
import jax.numpy as jnp
from jax import lax
from jax.experimental import pallas as pl
from jax.experimental.pallas import tpu as pltpu
from jax.sharding import PartitionSpec as P

MESH = pl.DeviceIdType.MESH
F32, BF16 = jnp.float32, jnp.bfloat16
ABSENT = -(2.0 ** 100)
K = 512


def dot(a, b):
    return jnp.dot(a, b, preferred_element_type=F32)


def iota(shape, axis):
    return lax.broadcasted_iota(jnp.int32, shape, axis)


def halves(x):
    high = x.astype(BF16)
    return high, (x - high.astype(F32)).astype(BF16)


def thirds(x):
    high, rest = x.astype(BF16), None
    rest = x - high.astype(F32)
    mid = rest.astype(BF16)
    return high, mid, (rest - mid.astype(F32)).astype(BF16)


def pick(onehot, x):
    y = dot(onehot, jnp.concatenate(thirds(x), axis=1))
    n = x.shape[1]
    return y[:, :n] + (y[:, n:2 * n] + y[:, 2 * n:])


def kernel(
    q_hbm, db_hbm, frames, shard_hbm, local_hbm, one_hbm, two_hbm, three_hbm, out_hbm,
    coarse_ref, refined_ref,
    qbuf, dbraw, dba, dbb, fmap, lens, msg, rbuf, cbuf, perm,
    shard_v, local_v, one_v, two_v, three_v, out_v,
    w1, w2, w3, x1, x2h, x2l, pen, best,
    send_sem, recv_sem, msg_send, msg_recv, local_sem,
):
    index, rep = lax.axis_index("index"), lax.axis_index("rep")
    c, y, xh, z = index % 2, (index // 2) % 4, (index // 8) % 2, index // 16
    x = xh * 2 + rep
    a, b = y // 2, ((y + 1) // 2) % 2
    ell = rep

    def device(z, x, y, c):
        return (((z * 2 + x // 2) * 4 + y) * 2 + c, x % 2)

    def y_of(a, b):
        return a * 3 + b * (1 - 2 * a)

    me_q = z * 4 + a * 2 + c
    me_b = xh * 2 + b
    b_own, b_q, b_r, b_s = me_b, (1 - xh) * 2 + b, xh * 2 + (1 - b), (1 - xh) * 2 + (1 - b)
    dev = {
        "+": device((z + 1) % 8, x, y, c),
        "-": device((z + 7) % 8, x, y, c),
        "a": device(z, x, 3 - y, c),
        "b": device(z, x, y_of(a, 1 - b), c),
        "d": device(z, x, y, 1 - c),
        "xh": device(z, 3 - x, y, c),
        "xl": device(z, xh * 2 + (1 - rep), y, c),
        "c1": device(z, (1 - xh) * 2 + rep, y, c),
        "c3": device(z, (1 - xh) * 2 + rep, y_of(a, 1 - b), c),
    }

    def row_device(k, da, dc):
        off = ((k + 1) // 2) * (1 - 2 * (k % 2))
        zk, ak, ck = (z + off + 8) % 8, (a + da) % 2, (c + dc) % 2
        return zk, ak, ck, device(zk, x, y_of(ak, b), ck)

    barrier = pltpu.get_barrier_semaphore()
    for target in dev.values():
        pl.semaphore_signal(barrier, inc=1, device_id=target, device_id_type=MESH)

    loads = [
        pltpu.make_async_copy(src, dst, local_sem.at[i])
        for i, (src, dst) in enumerate((
            (q_hbm, qbuf.at[me_q]),
            (db_hbm, dbraw.at[pl.ds(me_b * 4, 4)]),
            (three_hbm, three_v),
            (two_hbm, two_v),
            (one_hbm, one_v),
            (shard_hbm, shard_v),
            (local_hbm, local_v),
            (out_hbm, out_v),
        ))
    ]
    for load in loads:
        load.start()

    row8 = iota((8, 128), 0)
    own_lens = jnp.zeros((8, 128), F32)
    for u in range(4):
        own_lens = jnp.where(row8 == u, frames[u].astype(F32), own_lens)
    lens[me_b] = own_lens

    ids, started = {}, []

    def copy(name, src, dst, target):
        sem = ids.setdefault(name, len(ids))
        return pltpu.make_async_remote_copy(
            src_ref=src, dst_ref=dst, send_sem=send_sem.at[sem], recv_sem=recv_sem.at[sem],
            device_id=target, device_id_type=MESH,
        )

    def send(name, src, dst, target):
        started.append(copy(name, src, dst, target))
        started[-1].start()

    def wait(name, dst):
        copy(name, dst, dst, dev["d"]).wait_recv()

    def z_at(k):
        return (z + ((k + 1) // 2) * (1 - 2 * (k % 2)) + 8) % 8

    def half(zz, aa, h):
        return qbuf.at[zz * 4 + aa * 2 + c, pl.ds(h * 64, 64), :]

    def unit(zz, aa, cc):
        return qbuf.at[zz * 4 + aa * 2 + cc]

    def db_unit(block, u):
        return dbraw.at[block * 4 + u]

    pl.semaphore_wait(barrier, len(dev))

    def ring_send(way, d, item):
        k = 2 * (d - 1) - (1 if way == "+" else 0) if d > 1 else 0
        zz = z_at(k)
        ref = half(zz, 1 - a, 0) if item == 2 else half(zz, a, item)
        src = q_hbm.at[pl.ds(item * 64, 64), :] if d == 1 and item < 2 else ref
        send((way, d, item), src, ref, dev[way])

    def ring_wait(way, d, item):
        zz = z_at(2 * d - (1 if way == "+" else 0))
        wait((way, d, item), half(zz, 1 - a, 0) if item == 2 else half(zz, a, item))

    for h in range(2):
        ring_send("+", 1, 1 - h)
        ring_send("-", 1, 1 - h)
        send(("a", 0, h), q_hbm.at[pl.ds(h * 64, 64), :], half(z, a, h), dev["a"])

    def db_send(link, position):
        u = (2 * (1 - ell) + 1 + (3 * (position % 2)) + 2 * (position // 2)) % 4 if link == "xh" else (
            2 * (1 - ell) + position) % 4
        send((link, position), db_hbm.at[u], db_unit(me_b, u), dev[link])

    def db_wait(link, position):
        u = (2 * ell + 1 + (3 * (position % 2)) + 2 * (position // 2)) % 4 if link == "xh" else (
            2 * (1 - ell) + position) % 4
        wait((link, position), db_unit(b_q if link == "xh" else b_r, u))

    for position in range(2):
        db_send("xh", position)
        db_send("b", position)
    send(("d", 0, 0), q_hbm, unit(z, a, c), dev["d"])
    for name in ("b", "c1", "c3"):
        send(("len", name), lens.at[me_b], lens.at[me_b], dev[name])

    ri, ci = iota((256, 256), 0), iota((256, 256), 1)
    perm[...] = jnp.where(
        ci == (ri % 2) * 128 + ((ri // 2) % 8) * 16 + ri // 16, 1.0, 0.0
    ).astype(BF16)

    def permute(hb, first, second):
        raw = jnp.concatenate([dbraw[first[0] * 4 + first[1]], dbraw[second[0] * 4 + second[1]]], axis=0)
        rows = dot(perm[...], raw).astype(BF16)
        for u in range(16):
            piece = rows[u * 16:(u + 1) * 16]
            if hb < 4:
                at = (u % 4) * 64 + hb * 16
                dba[u // 4, at:at + 16, :] = piece
            else:
                at = (u % 8) * 32 + (hb % 2) * 16
                dbb[hb // 2 - 2, u // 8, at:at + 16, :] = piece

    lane = iota((8, 128), 1)

    def tile(group, k):
        zz = z_at(k)
        left = qbuf[pl.ds(zz * 4, 4)].reshape(512, K)
        top = None
        for t in range(4 if group == 0 else 2):
            right = dba[t] if group == 0 else dbb[group - 1, t]
            sim = lax.dot_general(left, right, (((1,), (1,)), ((), ())), preferred_element_type=F32)
            sim = jnp.maximum(sim[:, :128], sim[:, 128:])
            top = sim if top is None else jnp.maximum(top, sim)
        top = jnp.maximum(top, pltpu.roll(top, 64, 1))
        if group:
            top = jnp.maximum(top, pltpu.roll(top, 32, 1))
        mean = jnp.sum(top.reshape(32, 16, 128), axis=1).reshape(4, 8, 128)
        at = pl.ds(zz * 4, 4)
        if group:
            mean = jnp.where((lane // 32 == group + 1)[None], mean, fmap[at])
        fmap[at] = mean

    order = {
        "own": ((0, 0), (0, 1), (1, 0), (1, 1)),
        "q": ((3, 0), (2, 0), (6, 0), (5, 0)),
        "r": ((5, 1), (6, 1), (2, 1), (3, 1)),
        "s": ((4, 0), (4, 1), (7, 0), (7, 1)),
    }
    blocks = {"own": b_own, "q": b_q, "r": b_r, "s": b_s}

    def unit_of(name, i):
        return i if name == "own" else (2 * ell + i) % 4

    def length_lanes():
        total = jnp.zeros((1, 128), F32)
        lane1 = iota((1, 128), 1)
        for name, places in order.items():
            for i, (hb, v) in enumerate(places):
                value = lens[blocks[name], pl.ds(unit_of(name, i), 1), :]
                total = jnp.where((lane1 // 16 == hb) & (lane1 % 2 == v), value, total)
        return (lane1 % 16 // 2).astype(F32) < total

    def post(k, first):
        zz = z_at(k)
        rows = jnp.zeros((8, 128), F32)
        for i in range(4):
            maps = fmap[zz * 4 + i] * (K ** -0.5 / 16)
            maps = jnp.where(present, maps, ABSENT)
            msg[zz * 4 + i] = maps
            for shift in (8, 4, 2):
                maps = jnp.maximum(maps, pltpu.roll(maps, 128 - shift, 1))
            rows = jnp.where(row8 == i, jnp.sum(maps, axis=0, keepdims=True), rows)
        cbuf[me_b, zz] = rows
        for da in range(2):
            for dc in range(2):
                zk, ak, ck, target = row_device(k, da, dc)
                slot = zk * 4 + ak * 2 + ck
                if first and da == 0 and dc == 0:
                    rbuf[me_q] = msg[slot]
                else:
                    sem = k * 4 + da * 2 + dc
                    pltpu.make_async_remote_copy(
                        src_ref=msg.at[slot], dst_ref=rbuf.at[me_q], send_sem=msg_send.at[sem],
                        recv_sem=msg_recv.at[sem], device_id=target, device_id_type=MESH,
                    ).start()

    def weights_three():
        loads[2].wait()
        zero = jnp.zeros((64, 128), F32)
        for i in range(3):
            w = [three_v[(i * 3 + j) * 64:(i * 3 + j + 1) * 64, :] for j in range(3)]
            for r, (left, right) in enumerate(((w[1], w[0]), (w[2], w[1]), (zero, w[2]), (w[0], zero))):
                for s, part in enumerate((left, right)):
                    high, low = halves(part)
                    for at, value in ((0, high), (256, high), (512, low)):
                        at = i * 768 + at + r * 64
                        w3[at:at + 64, s * 128:(s + 1) * 128] = value

    def weights_rest():
        loads[3].wait()
        loads[4].wait()
        place = [jnp.where(iota((64, 128), 1) == iota((64, 128), 0) + 64 * s, 1.0, 0.0).astype(BF16) for s in range(2)]
        zero = jnp.zeros((32, 64), F32)
        for i in range(3):
            w = [two_v[(i * 3 + j) * 32:(i * 3 + j + 1) * 32, :] for j in range(3)]
            stacks = (jnp.concatenate(w + [zero], axis=0), jnp.concatenate([zero] + w, axis=0))
            for part in range(2):
                value = sum(dot(halves(stack)[part], where) for stack, where in zip(stacks, place)).astype(BF16)
                for r in range(2):
                    w2[i * 256 + r * 128:i * 256 + (r + 1) * 128, part * 128:(part + 1) * 128] = value
        spread = jnp.where(iota((32, 512), 1) % 32 == iota((32, 512), 0), 1.0, 0.0).astype(BF16)
        w1[...] = jnp.zeros((256, 512), BF16)
        j, col = iota((32, 512), 0), iota((32, 512), 1)
        g = (j % 16) // 2
        pos = 2 * (col // 128) - 1 + (col % 128) // 32
        for part in range(2):
            for i in range(3):
                value = jnp.zeros((32, 512), F32)
                for s in range(3):
                    line = dot(halves(jnp.broadcast_to(one_v[i, s], (16, 32)))[part], spread)[0:1]
                    hit = (g - pos + 1 == s) & (pos >= 0) & (pos < 8) & (j % 2 == 0)
                    value = value + jnp.where(hit, line, 0.0)
                w1[part * 128 + i * 32:part * 128 + (i + 1) * 32, :] = value.astype(BF16)

    def clear():
        none = jnp.zeros((128, 256), BF16)
        for p in range(4):
            x1[p, 0] = none
            x1[p, 9] = none
        for p in range(6):
            x2h[p, 0] = none
            x2h[p, 9] = none
            x2l[p, 0] = none
            x2l[p, 9] = none

        def edge(f, _):
            side = jnp.zeros((128, 128), BF16)
            x2h[1, f, :, 128:256] = side
            x2l[1, f, :, 128:256] = side
            x2h[4, f, :, 128:256] = side
            x2l[4, f, :, 128:256] = side
            return 0

        lax.fori_loop(1, 9, edge, 0)

    def share_other(k):
        zz = z_at(k)
        send(("d", k, 1), unit(zz, 1 - a, c), unit(zz, 1 - a, c), dev["d"])

    def slab_wait(k):
        zz = z_at(k)
        wait(("d", k, 0), unit(zz, a, 1 - c))
        wait(("d", k, 1), unit(zz, 1 - a, 1 - c))

    def main_item(d, item):
        for way in "+-" if d < 4 else "+":
            k = 2 * d - (1 if way == "+" else 0)
            zz = z_at(k)
            ring_wait(way, d, item)
            if d < 3 or (d == 3 and way == "+"):
                ring_send(way, d + 1, item)
            if item == 1:
                send(("a", k, 1), half(zz, a, 1), half(zz, a, 1), dev["a"])
            else:
                send(("d", k, 0), unit(zz, a, c), unit(zz, a, c), dev["d"])

    def other_item(d):
        for way in "+-" if d < 4 else "-":
            ring_wait(way, d, 2)
            if d < 3 or (d == 3 and way == "-"):
                ring_send(way, d + 1, 2)

    def partner_item(d):
        for k in (2 * d - 1, 2 * d) if d < 4 else (7,):
            wait(("a", k, 1), half(z_at(k), 1 - a, 1))
            share_other(k)

    q_units = [(b_q, (2 * ell + i) % 4) for i in (1, 0, 3, 2)]
    r_units = [(b_r, (2 * ell + i) % 4) for i in (2, 3, 0, 1)]
    s_units = [(b_s, (2 * ell + i) % 4) for i in range(4)]

    loads[0].wait()
    wait(("a", 0, 0), half(z, 1 - a, 0))
    for way in "+-":
        ring_send(way, 1, 2)
    loads[1].wait()
    permute(0, (b_own, 0), (b_own, 1))
    main_item(1, 1)
    permute(1, (b_own, 2), (b_own, 3))
    wait(("a", 0, 1), half(z, 1 - a, 1))
    share_other(0)
    main_item(1, 0)
    db_wait("xh", 0)
    send(("b", 4), db_unit(b_q, 2 * ell + 1), db_unit(b_q, 2 * ell + 1), dev["b"])
    db_wait("b", 0)
    send(("xh", 4), db_unit(b_r, 2 * (1 - ell)), db_unit(b_r, 2 * (1 - ell)), dev["xh"])
    db_send("xh", 2)
    db_send("b", 2)
    permute(2, q_units[0], r_units[0])
    other_item(1)
    weights_three()
    partner_item(1)
    db_wait("xh", 1)
    db_wait("b", 1)
    db_send("xh", 3)
    db_send("b", 3)
    permute(3, q_units[1], r_units[1])
    main_item(2, 1)
    slab_wait(0)
    tile(0, 0)
    main_item(2, 0)
    slab_wait(1)
    slab_wait(2)
    tile(0, 1)
    other_item(2)
    tile(0, 2)
    weights_rest()
    partner_item(2)
    wait(("b", 4), db_unit(b_s, 2 * ell + 1))
    wait(("xh", 4), db_unit(b_s, 2 * ell))
    for i in range(2):
        send(("xl", i), db_unit(b_s, 2 * ell + i), db_unit(b_s, 2 * ell + i), dev["xl"])
    permute(4, s_units[0], s_units[1])
    main_item(3, 1)
    clear()
    slab_wait(3)
    tile(0, 3)
    slab_wait(4)
    tile(0, 4)
    for name, block in (("b", b_r), ("c1", b_q), ("c3", b_s)):
        wait(("len", name), lens.at[block])
    present = length_lanes()
    main_item(3, 0)
    db_wait("xh", 2)
    db_wait("b", 2)
    permute(5, q_units[2], r_units[2])
    tile(1, 0)
    tile(1, 1)
    other_item(3)
    tile(1, 2)
    partner_item(3)
    tile(1, 3)
    tile(1, 4)
    slab_wait(5)
    tile(0, 5)
    main_item(4, 1)
    tile(1, 5)
    slab_wait(6)
    tile(0, 6)
    tile(1, 6)
    db_wait("xh", 3)
    db_wait("b", 3)
    permute(6, q_units[3], r_units[3])
    for i in range(2):
        wait(("xl", i), db_unit(b_s, 2 * (1 - ell) + i))
    permute(7, s_units[2], s_units[3])
    main_item(4, 0)
    tile(2, 0)
    tile(2, 1)
    other_item(4)
    partner_item(4)
    for k in range(2, 7):
        tile(2, k)
    slab_wait(7)
    tile(0, 7)
    tile(1, 7)
    tile(2, 7)
    post(0, True)

    def post_loop(k, _):
        post(k, False)
        return 0

    lax.fori_loop(1, 8, post_loop, 0)
    ri, ci = iota((128, 128), 0), iota((128, 128), 1)
    where = ri < 0
    for r, (name, places) in enumerate(order.items()):
        for i, (hb, v) in enumerate(places):
            where = where | ((ri == hb * 16 + v) & (ci == r * 32 + unit_of(name, i)))
    sums = cbuf[me_b].reshape(64, 128)
    where = jnp.where(where, 1.0, 0.0).astype(BF16)
    sums = sum(dot(part, where) for part in thirds(sums)) * 0.125
    cbuf[me_b] = sums.reshape(8, 8, 128)
    for name in ("b", "c1", "c3"):
        send(("coarse", name), cbuf.at[me_b], cbuf.at[me_b], dev[name])

    def column(row):
        return jnp.sum(
            jnp.where(iota((128, 128), 0) == iota((128, 128), 1), row.astype(F32), 0.0), axis=1, keepdims=True
        ).astype(jnp.int32)

    for i in (5, 6, 7):
        loads[i].wait()
    shard, place = column(shard_v[...]), column(local_v[...])
    cy = (shard // 2) % 4
    ca, cb = cy // 2, ((cy + 1) // 2) % 2
    source = (shard // 16) * 4 + ca * 2 + shard % 2
    cross, other = ((shard // 8) % 2) != xh, cb != b
    offset = (place + 2 * ell) % 4
    chb, cv = place // 2, place % 2
    for rule, name in ((cross & ~other, "q"), (other & ~cross, "r"), (cross & other, "s")):
        for i, (hb, v) in enumerate(order[name]):
            hit = rule & (offset == i)
            chb, cv = jnp.where(hit, hb, chb), jnp.where(hit, v, cv)
    cshift = chb * 16 + cv
    cols = iota((128, 96), 1)
    onehot = jnp.where(cols % 32 == source, 1.0, 0.0).astype(BF16)

    def msg_copy(k, da, dc):
        off = ((k + 1) // 2) * (1 - 2 * (k % 2))
        slot = ((z - off + 8) % 8) * 4 + ((a + da) % 2) * 2 + (c + dc) % 2
        sem = k * 4 + da * 2 + dc
        return pltpu.make_async_remote_copy(
            src_ref=msg.at[slot], dst_ref=rbuf.at[slot], send_sem=msg_send.at[sem],
            recv_sem=msg_recv.at[sem], device_id=dev["d"], device_id_type=MESH,
        )

    def msg_wait(t, _):
        msg_copy(t // 4, (t // 2) % 2, t % 2).wait_recv()
        return 0

    lax.fori_loop(1, 32, msg_wait, 0)
    lane = iota((128, 128), 1)
    kept = (lane < 16) & (lane % 2 == 0)
    near = []
    for f in range(8):
        t = dot(onehot, jnp.concatenate(thirds(rbuf[:, f, :]), axis=0))
        for bit in (64, 32, 16, 1):
            t = jnp.where((cshift // bit) % 2 == 1, pltpu.roll(t, 128 - bit, 1), t)
        there = t > ABSENT / 2
        if f == 0:
            gap = jnp.where(there, 0.0, -3e38)
            for g in range(8):
                pen[g] = gap[:, 2 * g:2 * g + 1]
        t = jnp.where(there & kept, t, 0.0)
        high = t.astype(BF16).astype(F32)
        near.append(high + pltpu.roll(t - high, 16, 1))
    for f in range(8):
        around = pltpu.roll(near[f], 32, 1)
        if f > 0:
            around = around + near[f - 1]
        if f < 7:
            around = around + pltpu.roll(near[f + 1], 64, 1)
        around = around.astype(BF16)
        out = jnp.maximum(dot(jnp.concatenate([around, around], axis=1), w1[...]), 0.0)
        high1, low1 = halves(out)
        for p in range(4):
            x1[p, f + 1, :, 0:128] = high1[:, p * 128:(p + 1) * 128]
            x1[p, f + 1, :, 128:256] = low1[:, p * 128:(p + 1) * 128]

    def second(p, _):
        out = dot(jnp.concatenate([x1[p, i:i + 8].reshape(1024, 256) for i in range(3)], axis=1), w2[...])
        out = jnp.maximum(out[:, :128] + out[:, 128:], 0.0)
        for ref, part in zip((x2h, x2l), halves(out)):
            part = part.reshape(8, 128, 128)
            ref[p + 1, 1:9, :, 0:128] = part
            ref[p, 1:9, :, 128:192] = part[:, :, 0:64]
            ref[p + 2, 1:9, :, 192:256] = part[:, :, 64:128]
        return 0

    lax.fori_loop(0, 4, second, 0)
    scale = jnp.concatenate([out_v[...], out_v[...]], axis=1)
    best[...] = jnp.full((1024, 1), -3e38, F32)

    def third(p, _):
        parts = []
        for i in range(3):
            upper = x2h[p + 1, i:i + 8].reshape(1024, 256)
            parts += [upper, x2l[p + 1, i:i + 8].reshape(1024, 256), upper]
        out = dot(jnp.concatenate(parts, axis=1), w3[...])
        out = jnp.maximum(out, 0.0) * scale
        for s in range(2):
            total = jnp.sum(out[:, s * 128:(s + 1) * 128], axis=1, keepdims=True)
            total = total.reshape(8, 128, 1) + pen[2 * p + s][None]
            best[...] = jnp.maximum(best[...], total.reshape(1024, 1))
        return 0

    lax.fori_loop(0, 4, third, 0)
    mean = jnp.sum(best[...].reshape(8, 128, 1), axis=0) * 0.125
    refined_ref[...] = jnp.sum(
        jnp.where(iota((128, 128), 0) == iota((128, 128), 1), mean, 0.0), axis=0, keepdims=True
    )

    for name, block in (("b", b_r), ("c1", b_q), ("c3", b_s)):
        wait(("coarse", name), cbuf.at[block])
    n, col = iota((128, 256), 0), iota((128, 256), 1)
    ny = (n // 2) % 4
    nxh, nb = (n // 8) % 2, ((ny + 1) // 2) % 2
    want = (nxh * 2 + nb) * 64 + (n // 16) * 8 + (ny // 2) * 2 + n % 2
    scores = pick(jnp.where(col == want, 1.0, 0.0).astype(BF16), cbuf[...].reshape(256, 128))
    relation = (nxh != xh).astype(jnp.int32)[:, :128] + 2 * (nb != b).astype(jnp.int32)[:, :128]
    mine = scores
    for r in range(1, 4):
        mine = jnp.where(relation == r, pltpu.roll(scores, 128 - 32 * r, 1), mine)
    coarse_ref[...] = mine.T[0:4]

    for sent in started:
        sent.wait_send()

    def sent_wait(t, _):
        msg_copy(t // 4, (t // 2) % 2, t % 2).wait_send()
        return 0

    lax.fori_loop(1, 32, sent_wait, 0)


def local(queries, database, db_frames, cand_shard, cand_local, conv_one, conv_two, conv_three, conv_out):
    anywhere = pl.BlockSpec(memory_space=pltpu.HBM)
    vmem = pl.BlockSpec(memory_space=pltpu.VMEM)
    smem = pl.BlockSpec(memory_space=pltpu.SMEM)
    coarse, refined = pl.pallas_call(
        kernel,
        out_shape=(jax.ShapeDtypeStruct((4, 128), F32), jax.ShapeDtypeStruct((1, 128), F32)),
        in_specs=[anywhere, anywhere, smem] + [anywhere] * 6,
        out_specs=(vmem, vmem),
        scratch_shapes=[
            pltpu.VMEM((32, 128, K), BF16),
            pltpu.VMEM((16, 128, K), BF16),
            pltpu.VMEM((4, 256, K), BF16),
            pltpu.VMEM((2, 2, 256, K), BF16),
            pltpu.VMEM((32, 8, 128), F32),
            pltpu.VMEM((4, 8, 128), F32),
            pltpu.VMEM((32, 8, 128), F32),
            pltpu.VMEM((32, 8, 128), F32),
            pltpu.VMEM((4, 8, 8, 128), F32),
            pltpu.VMEM((256, 256), BF16),
            pltpu.VMEM((1, 128), jnp.int32),
            pltpu.VMEM((1, 128), jnp.int32),
            pltpu.VMEM((3, 3, 1, 32), F32),
            pltpu.VMEM((288, 64), F32),
            pltpu.VMEM((576, 128), F32),
            pltpu.VMEM((1, 128), F32),
            pltpu.VMEM((256, 512), BF16),
            pltpu.VMEM((768, 256), BF16),
            pltpu.VMEM((2304, 256), BF16),
            pltpu.VMEM((4, 10, 128, 256), BF16),
            pltpu.VMEM((6, 10, 128, 256), BF16),
            pltpu.VMEM((6, 10, 128, 256), BF16),
            pltpu.VMEM((8, 128, 1), F32),
            pltpu.VMEM((1024, 1), F32),
            pltpu.SemaphoreType.DMA((72,)),
            pltpu.SemaphoreType.DMA((72,)),
            pltpu.SemaphoreType.DMA((32,)),
            pltpu.SemaphoreType.DMA((32,)),
            pltpu.SemaphoreType.DMA((8,)),
        ],
        compiler_params=pltpu.CompilerParams(
            collective_id=0, has_side_effects=True, vmem_limit_bytes=64 * 1024 * 1024
        ),
        cost_estimate=pl.CostEstimate(flops=13_000_000_000, bytes_accessed=2_000_000, transcendentals=0),
    )(
        queries.reshape(128, K), database.reshape(4, 128, K), db_frames, cand_shard.reshape(1, 128),
        cand_local.reshape(1, 128), conv_one, conv_two.reshape(288, 64),
        conv_three.reshape(576, 128), conv_out.reshape(1, 128),
    )
    return coarse.T[None], refined[None]


def solution(mesh):
    in_specs = (
        P("index", "rep", None, None, None),
        P("index", None, None, None),
        P("index"),
        P("index", "rep", None, None),
        P("index", "rep", None),
        P(),
        P(),
        P(),
        P(),
    )
    out_specs = (P("rep", None, "index"), P("index", "rep", None))
    return jax.shard_map(local, mesh=mesh, in_specs=in_specs, out_specs=out_specs, check_vma=False)
```

```python
import functools

import jax
import jax.numpy as jnp
from jax import lax
from jax.experimental import pallas as pl
from jax.experimental.pallas import tpu as pltpu
from jax.sharding import PartitionSpec as P

MESH = pl.DeviceIdType.MESH
F32, BF16 = jnp.float32, jnp.bfloat16
ABSENT = -(2.0 ** 100)
K = 512
ORDER = (
    ("permute", 0), ("permute", 1), ("prepare", 0), ("prepare", 1), ("prepare", 2), ("get", "d", (0, 0)),
    ("prepare", 3), ("prepare", 4), ("prepare", 5), ("prepare", 6), ("prepare", 7), ("prepare", 8), ("prepare", 9),
    ("prepare", 10), ("prepare", 11), ("prepare", 12), ("get", "a", 0), ("put", "+", (1, 2)), ("put", "-", (1, 2)),
    ("get", "+", (1, 1)), ("put", "+", (2, 1)), ("put", "a", 2), ("get", "-", (1, 1)), ("put", "-", (2, 1)),
    ("put", "a", 3), ("get", "a", 1), ("put", "d", (0, 1)), ("get", "+", (1, 0)), ("put", "+", (2, 0)),
    ("put", "d", (1, 0)), ("get", "-", (1, 0)), ("put", "-", (2, 0)), ("put", "d", (2, 0)), ("get", "xh", 0),
    ("put", "xl", 0), ("get", "b", 0), ("put", "xh", 4), ("put", "b", 4), ("put", "xl", 1), ("permute", 2),
    ("get", "d", (0, 1)), ("tile", 0, 0), ("get", "d", (1, 0)), ("lengths",), ("get", "d", (2, 0)),
    ("get", "+", (1, 2)), ("put", "+", (2, 2)), ("get", "-", (1, 2)), ("put", "-", (2, 2)), ("get", "xh", 1),
    ("get", "a", 2), ("put", "d", (1, 1)), ("get", "b", 1), ("put", "xh", 5), ("put", "b", 5), ("permute", 3),
    ("tile", 1, 0), ("get", "+", (2, 1)), ("put", "+", (3, 1)), ("put", "a", 4), ("get", "-", (2, 1)),
    ("put", "-", (3, 1)), ("put", "a", 5), ("get", "d", (1, 1)), ("get", "a", 3), ("put", "d", (2, 1)),
    ("tile", 0, 1), ("tile", 1, 1), ("get", "+", (2, 0)), ("put", "+", (3, 0)), ("put", "d", (3, 0)),
    ("get", "-", (2, 0)), ("put", "-", (3, 0)), ("put", "d", (4, 0)), ("get", "d", (2, 1)), ("get", "xl", 0),
    ("get", "xh", 4), ("put", "xh", 2), ("get", "b", 4), ("put", "b", 2), ("permute", 4), ("tile", 0, 2),
    ("tile", 1, 2), ("get", "d", (3, 0)), ("get", "+", (2, 2)), ("put", "+", (3, 2)), ("get", "-", (2, 2)),
    ("put", "-", (3, 2)), ("get", "d", (4, 0)), ("get", "a", 4), ("put", "d", (3, 1)), ("get", "+", (3, 1)),
    ("put", "+", (4, 1)), ("put", "a", 6), ("get", "-", (3, 1)), ("put", "a", 7), ("get", "xl", 1), ("get", "xh", 5),
    ("get", "b", 5), ("permute", 5), ("permute", 6), ("tile", 2, 0), ("tile", 2, 1), ("get", "d", (3, 1)),
    ("get", "a", 5), ("put", "d", (4, 1)), ("get", "+", (3, 0)), ("put", "+", (4, 0)), ("put", "d", (5, 0)),
    ("get", "-", (3, 0)), ("put", "d", (6, 0)), ("tile", 2, 2), ("tile", 0, 3), ("tile", 1, 3), ("tile", 2, 3),
    ("get", "d", (4, 1)), ("get", "+", (3, 2)), ("get", "-", (3, 2)), ("put", "-", (4, 2)), ("get", "d", (5, 0)),
    ("tile", 0, 4), ("get", "xh", 2), ("get", "d", (6, 0)), ("get", "b", 2), ("permute", 7), ("tile", 3, 0),
    ("post", 0), ("get", "+", (4, 1)), ("put", "a", 8), ("get", "a", 6), ("put", "d", (5, 1)), ("tile", 3, 1),
    ("post", 1), ("tile", 3, 2), ("post", 2), ("tile", 3, 3), ("get", "d", (5, 1)), ("get", "a", 7),
    ("put", "d", (6, 1)), ("get", "+", (4, 0)), ("put", "d", (7, 0)), ("post", 3), ("tile", 1, 4), ("tile", 2, 4),
    ("tile", 3, 4), ("get", "d", (6, 1)), ("post", 4), ("get", "-", (4, 2)), ("get", "d", (7, 0)), ("tile", 0, 5),
    ("tile", 1, 5), ("tile", 2, 5), ("tile", 3, 5), ("get", "a", 8), ("put", "d", (7, 1)), ("post", 5),
    ("tile", 0, 6), ("tile", 1, 6), ("tile", 2, 6), ("tile", 3, 6), ("get", "d", (7, 1)), ("post", 6), ("tile", 0, 7),
    ("tile", 1, 7), ("tile", 2, 7), ("tile", 3, 7), ("post", 7),
)


def dot(a, b):
    return jnp.dot(a, b, preferred_element_type=F32)


def iota(shape, axis):
    return lax.broadcasted_iota(jnp.int32, shape, axis)


def halves(x):
    high = x.astype(BF16)
    return high, (x - high.astype(F32)).astype(BF16)


def thirds(x):
    high, rest = x.astype(BF16), None
    rest = x - high.astype(F32)
    mid = rest.astype(BF16)
    return high, mid, (rest - mid.astype(F32)).astype(BF16)


def pick(onehot, x):
    y = dot(onehot, jnp.concatenate(thirds(x), axis=1))
    n = x.shape[1]
    return y[:, :n] + (y[:, n:2 * n] + y[:, 2 * n:])


def kernel(
    q_hbm, db_hbm, frames, shard_hbm, local_hbm, one_hbm, two_hbm, three_hbm, out_hbm,
    coarse_ref, refined_ref,
    qbuf, dbraw, dbp, fmap, lens, msg, rbuf, cbuf, perm,
    shard_v, local_v, one_v, two_v, three_v, out_v,
    w1, w2, w3, x1, x2h, x2l, products, pen,
    send_sem, recv_sem, msg_send, msg_recv, local_sem,
):
    index, rep = lax.axis_index("index"), lax.axis_index("rep")
    c, y, xh, z = index % 2, (index // 2) % 4, (index // 8) % 2, index // 16
    x = xh * 2 + rep
    a, b = y // 2, ((y + 1) // 2) % 2
    ell = rep

    def device(z, x, y, c):
        return (((z * 2 + x // 2) * 4 + y) * 2 + c, x % 2)

    def y_of(a, b):
        return a * 3 + b * (1 - 2 * a)

    me_q = z * 4 + a * 2 + c
    me_b = xh * 2 + b
    b_own, b_q, b_r, b_s = me_b, (1 - xh) * 2 + b, xh * 2 + (1 - b), (1 - xh) * 2 + (1 - b)
    dev = {
        "+": device((z + 1) % 8, x, y, c),
        "-": device((z + 7) % 8, x, y, c),
        "a": device(z, x, 3 - y, c),
        "b": device(z, x, y_of(a, 1 - b), c),
        "d": device(z, x, y, 1 - c),
        "xh": device(z, 3 - x, y, c),
        "xl": device(z, xh * 2 + (1 - rep), y, c),
        "c1": device(z, (1 - xh) * 2 + rep, y, c),
        "c3": device(z, (1 - xh) * 2 + rep, y_of(a, 1 - b), c),
    }

    def row_device(k, da, dc):
        off = ((k + 1) // 2) * (1 - 2 * (k % 2))
        zk, ak, ck = (z + off + 8) % 8, (a + da) % 2, (c + dc) % 2
        return zk, ak, ck, device(zk, x, y_of(ak, b), ck)

    barrier = pltpu.get_barrier_semaphore()
    for target in dev.values():
        pl.semaphore_signal(barrier, inc=1, device_id=target, device_id_type=MESH)

    loads = [
        pltpu.make_async_copy(src, dst, local_sem.at[i])
        for i, (src, dst) in enumerate((
            (q_hbm, qbuf.at[me_q]),
            (db_hbm, dbraw.at[pl.ds(me_b * 4, 4)]),
            (three_hbm, three_v),
            (two_hbm, two_v),
            (one_hbm, one_v),
            (shard_hbm, shard_v),
            (local_hbm, local_v),
            (out_hbm, out_v),
        ))
    ]
    for load in loads:
        load.start()

    row8 = iota((8, 128), 0)
    own_lens = jnp.zeros((8, 128), F32)
    for u in range(4):
        own_lens = jnp.where(row8 == u, frames[u].astype(F32), own_lens)
    lens[me_b] = own_lens

    ids, started = {}, []

    def copy(name, src, dst, target):
        sem = ids.setdefault(name, len(ids))
        return pltpu.make_async_remote_copy(
            src_ref=src, dst_ref=dst, send_sem=send_sem.at[sem], recv_sem=recv_sem.at[sem],
            device_id=target, device_id_type=MESH,
        )

    def send(name, src, dst, target):
        started.append(copy(name, src, dst, target))
        started[-1].start()

    def wait(name, dst):
        copy(name, dst, dst, dev["d"]).wait_recv()

    def z_at(k):
        return (z + ((k + 1) // 2) * (1 - 2 * (k % 2)) + 8) % 8

    def half(zz, aa, h):
        return qbuf.at[zz * 4 + aa * 2 + c, pl.ds(h * 64, 64), :]

    def unit(zz, aa, cc):
        return qbuf.at[zz * 4 + aa * 2 + cc]

    def db_unit(block, u):
        return dbraw.at[block * 4 + u]

    pl.semaphore_wait(barrier, len(dev))

    def ring_send(way, d, item):
        k = 2 * (d - 1) - (1 if way == "+" else 0) if d > 1 else 0
        zz = z_at(k)
        ref = half(zz, 1 - a, 0) if item == 2 else half(zz, a, item)
        src = q_hbm.at[pl.ds(item * 64, 64), :] if d == 1 and item < 2 else ref
        send((way, d, item), src, ref, dev[way])

    def ring_wait(way, d, item):
        zz = z_at(2 * d - (1 if way == "+" else 0))
        wait((way, d, item), half(zz, 1 - a, 0) if item == 2 else half(zz, a, item))

    def db_at(link, position):
        first = {"xh": (2, 3, 1, None, 0, 1), "b": (2, 3, 1, None, 2, 3)}[link]
        block = b_s if position > 3 else b_q if link == "xh" else b_r
        return block, (2 * ell + first[position]) % 4

    def put(link, key):
        name = (link, key)
        if link in "+-":
            ring_send(link, *key)
        elif link == "a":
            if key < 2:
                send(name, q_hbm.at[pl.ds(key * 64, 64), :], half(z, a, key), dev["a"])
            else:
                ref = half(z_at(key - 1), a, 1)
                send(name, ref, ref, dev["a"])
        elif link == "d":
            k, other = key
            ref = unit(z_at(k), 1 - a if other else a, c)
            send(name, ref if k or other else q_hbm, ref, dev["d"])
        elif link == "xl":
            ref = db_unit(b_r if key else b_q, (2 * ell + 2) % 4)
            send(name, ref, ref, dev["xl"])
        elif key > 3:
            ref = db_unit(b_r if link == "xh" else b_q, (2 * ell + key - 2) % 4)
            send(name, ref, ref, dev[link])
        else:
            first = (0, 1, 3) if link == "xh" else (2, 3, 1)
            u = (2 * ell + first[key]) % 4
            send(name, db_hbm.at[u], db_unit(me_b, u), dev[link])

    def get(link, key):
        name = (link, key)
        if link in "+-":
            ring_wait(link, *key)
        elif link == "a":
            wait(name, half(z, 1 - a, key) if key < 2 else half(z_at(key - 1), 1 - a, 1))
        elif link == "d":
            wait(name, unit(z_at(key[0]), 1 - a if key[1] else a, 1 - c))
        elif link == "xl":
            wait(name, db_unit(b_r if key else b_q, 2 * ell))
        else:
            wait(name, db_unit(*db_at(link, key)))

    for link, keys in (
        ("+", ((1, 1),)), ("-", ((1, 1),)), ("a", (0,)), ("+", ((1, 0),)), ("-", ((1, 0),)), ("a", (1,)),
        ("xh", (0,)), ("b", (0,)), ("d", ((0, 0),)), ("xh", (1,)), ("b", (1,)),
    ):
        for key in keys:
            put(link, key)
    for name in ("b", "c1", "c3"):
        send(("len", name), lens.at[me_b], lens.at[me_b], dev[name])

    ri, ci = iota((256, 256), 0), iota((256, 256), 1)
    perm[...] = jnp.where(
        ci == (ri % 2) * 128 + ((ri // 2) % 8) * 16 + ri // 16, 1.0, 0.0
    ).astype(BF16)

    def permute(hb):
        videos = (
            ((b_own, 0), (b_own, 1)), ((b_own, 2), (b_own, 3)),
            (db_at("xh", 0), db_at("b", 0)), (db_at("xh", 1), db_at("b", 1)), (db_at("xh", 4), db_at("b", 4)),
            (db_at("xh", 5), db_at("b", 5)), ((b_q, 2 * ell), (b_r, 2 * ell)), (db_at("xh", 2), db_at("b", 2)),
        )[hb]
        raw = jnp.concatenate([dbraw[block * 4 + u] for block, u in videos], axis=0)
        rows = dot(perm[...], raw).astype(BF16)
        for u in range(16):
            at = (u % 8) * 32 + (hb % 2) * 16
            dbp[hb // 2, u // 8, at:at + 16, :] = rows[u * 16:(u + 1) * 16]

    lane = iota((8, 128), 1)

    def tile(group, k):
        zz = z_at(k)
        left = qbuf[pl.ds(zz * 4, 4)].reshape(512, K)
        top = None
        for t in range(2):
            sim = lax.dot_general(left, dbp[group, t], (((1,), (1,)), ((), ())), preferred_element_type=F32)
            sim = jnp.maximum(sim[:, :128], sim[:, 128:])
            top = sim if top is None else jnp.maximum(top, sim)
        top = jnp.maximum(top, pltpu.roll(top, 64, 1))
        top = jnp.maximum(top, pltpu.roll(top, 32, 1))
        mean = jnp.sum(top.reshape(32, 16, 128), axis=1).reshape(4, 8, 128)
        at = pl.ds(zz * 4, 4)
        if group:
            mean = jnp.where((lane // 32 == group)[None], mean, fmap[at])
        fmap[at] = mean

    order = {
        "own": ((0, 0), (0, 1), (1, 0), (1, 1)),
        "q": ((6, 0), (7, 0), (2, 0), (3, 0)),
        "r": ((6, 1), (7, 1), (2, 1), (3, 1)),
        "s": ((4, 0), (5, 0), (4, 1), (5, 1)),
    }
    blocks = {"own": b_own, "q": b_q, "r": b_r, "s": b_s}

    def unit_of(name, i):
        return i if name == "own" else (2 * ell + i) % 4

    def length_lanes():
        total = jnp.zeros((1, 128), F32)
        lane1 = iota((1, 128), 1)
        for name, places in order.items():
            for i, (hb, v) in enumerate(places):
                value = lens[blocks[name], pl.ds(unit_of(name, i), 1), :]
                total = jnp.where((lane1 // 16 == hb) & (lane1 % 2 == v), value, total)
        return (lane1 % 16 // 2).astype(F32) < total

    def post(k):
        zz = z_at(k)
        rows = jnp.zeros((8, 128), F32)
        for i in range(4):
            maps = fmap[zz * 4 + i] * (K ** -0.5 / 16)
            maps = jnp.where(present, maps, ABSENT)
            msg[zz * 4 + i] = maps
            for shift in (8, 4, 2):
                maps = jnp.maximum(maps, pltpu.roll(maps, 128 - shift, 1))
            rows = jnp.where(row8 == i, jnp.sum(maps, axis=0, keepdims=True), rows)
        cbuf[me_b, zz] = rows
        for da in range(2):
            for dc in range(2):
                zk, ak, ck, target = row_device(k, da, dc)
                slot = zk * 4 + ak * 2 + ck
                if k == 0 and da == 0 and dc == 0:
                    rbuf[me_q] = msg[slot]
                else:
                    sem = k * 4 + da * 2 + dc
                    pltpu.make_async_remote_copy(
                        src_ref=msg.at[slot], dst_ref=rbuf.at[me_q], send_sem=msg_send.at[sem],
                        recv_sem=msg_recv.at[sem], device_id=target, device_id_type=MESH,
                    ).start()

    def third_weights(j):
        zero = jnp.zeros((64, 128), F32)
        taps = [[three_v[(i * 3 + t) * 64:(i * 3 + t + 1) * 64, :] for i in range(3)] for t in range(3)]
        w = []
        for g0, g1, g2 in taps:
            w.append((g0, (g0 + g2 + g1) * 0.5, (g0 + g2 - g1) * 0.5, g2)[j])
        for r, (left, right) in enumerate(((w[1], w[0]), (w[2], w[1]), (zero, w[2]), (w[0], zero))):
            for s, part in enumerate((left, right)):
                high, low = halves(part)
                for at, value in ((0, high), (256, high), (512, low)):
                    at = j * 768 + at + r * 64
                    w3[at:at + 64, s * 128:(s + 1) * 128] = value

    def second_weights(i):
        place = [jnp.where(iota((64, 128), 1) == iota((64, 128), 0) + 64 * s, 1.0, 0.0).astype(BF16) for s in range(2)]
        zero = jnp.zeros((32, 64), F32)
        w = [two_v[(i * 3 + j) * 32:(i * 3 + j + 1) * 32, :] for j in range(3)]
        stacks = (jnp.concatenate(w + [zero], axis=0), jnp.concatenate([zero] + w, axis=0))
        for part in range(2):
            value = sum(dot(halves(stack)[part], where) for stack, where in zip(stacks, place)).astype(BF16)
            for r in range(2):
                w2[i * 256 + r * 128:i * 256 + (r + 1) * 128, part * 128:(part + 1) * 128] = value

    def first_weights(i):
        spread = jnp.where(iota((32, 512), 1) % 32 == iota((32, 512), 0), 1.0, 0.0).astype(BF16)
        j, col = iota((32, 512), 0), iota((32, 512), 1)
        g = (j % 16) // 2
        pos = 2 * (col // 128) - 1 + (col % 128) // 32
        for part in range(2):
            value = jnp.zeros((32, 512), F32)
            for s in range(3):
                line = dot(halves(jnp.broadcast_to(one_v[i, s], (16, 32)))[part], spread)[0:1]
                hit = (g - pos + 1 == s) & (pos >= 0) & (pos < 8) & (j % 2 == 0)
                value = value + jnp.where(hit, line, 0.0)
            w1[part * 128 + i * 32:part * 128 + (i + 1) * 32, :] = value.astype(BF16)
            if i == 0:
                w1[part * 128 + 96:part * 128 + 128, :] = jnp.zeros((32, 512), BF16)

    def clear_ends(ref):
        for p in range(4):
            for f in (0, 9):
                ref[p, f] = jnp.zeros((128, 256), BF16)

    def clear_sides(ref):
        for p in (1, 4):
            ref[p, :, :, 128:256] = jnp.zeros((16, 128, 128), BF16)

    def prepare(i):
        if i == 0:
            for load in (2, 3, 4):
                loads[load].wait()
        (
            *[functools.partial(third_weights, t) for t in range(4)],
            *[functools.partial(second_weights, t) for t in range(3)],
            *[functools.partial(first_weights, t) for t in range(3)],
            functools.partial(clear_ends, x1),
            *[functools.partial(clear_sides, ref) for ref in (x2h, x2l)],
        )[i]()

    present = None
    loads[0].wait()
    loads[1].wait()
    for step, *which in ORDER:
        if step == "lengths":
            for name, block in (("b", b_r), ("c1", b_q), ("c3", b_s)):
                wait(("len", name), lens.at[block])
            present = length_lanes()
        else:
            dict(get=get, put=put, permute=permute, tile=tile, post=post, prepare=prepare)[step](*which)
    ri, ci = iota((128, 128), 0), iota((128, 128), 1)
    where = ri < 0
    for r, (name, places) in enumerate(order.items()):
        for i, (hb, v) in enumerate(places):
            where = where | ((ri == hb * 16 + v) & (ci == r * 32 + unit_of(name, i)))
    sums = cbuf[me_b].reshape(64, 128)
    where = jnp.where(where, 1.0, 0.0).astype(BF16)
    sums = sum(dot(part, where) for part in thirds(sums)) * 0.125
    cbuf[me_b] = sums.reshape(8, 8, 128)
    for name in ("b", "c1", "c3"):
        send(("coarse", name), cbuf.at[me_b], cbuf.at[me_b], dev[name])

    def column(row):
        return jnp.sum(
            jnp.where(iota((128, 128), 0) == iota((128, 128), 1), row.astype(F32), 0.0), axis=1, keepdims=True
        ).astype(jnp.int32)

    for i in (5, 6, 7):
        loads[i].wait()
    shard, place = column(shard_v[...]), column(local_v[...])
    cy = (shard // 2) % 4
    ca, cb = cy // 2, ((cy + 1) // 2) % 2
    source = (shard // 16) * 4 + ca * 2 + shard % 2
    cross, other = ((shard // 8) % 2) != xh, cb != b
    offset = (place + 2 * ell) % 4
    chb, cv = place // 2, place % 2
    for rule, name in ((cross & ~other, "q"), (other & ~cross, "r"), (cross & other, "s")):
        for i, (hb, v) in enumerate(order[name]):
            hit = rule & (offset == i)
            chb, cv = jnp.where(hit, hb, chb), jnp.where(hit, v, cv)
    cshift = chb * 16 + cv
    cols = iota((128, 96), 1)
    onehot = jnp.where(cols % 32 == source, 1.0, 0.0).astype(BF16)

    def msg_copy(k, da, dc):
        off = ((k + 1) // 2) * (1 - 2 * (k % 2))
        slot = ((z - off + 8) % 8) * 4 + ((a + da) % 2) * 2 + (c + dc) % 2
        sem = k * 4 + da * 2 + dc
        return pltpu.make_async_remote_copy(
            src_ref=msg.at[slot], dst_ref=rbuf.at[slot], send_sem=msg_send.at[sem],
            recv_sem=msg_recv.at[sem], device_id=dev["d"], device_id_type=MESH,
        )

    def msg_wait(t, _):
        msg_copy(t // 4, (t // 2) % 2, t % 2).wait_recv()
        return 0

    lax.fori_loop(1, 32, msg_wait, 0)
    lane = iota((128, 128), 1)
    kept = (lane < 16) & (lane % 2 == 0)
    near = []
    for f in range(8):
        t = dot(onehot, jnp.concatenate(thirds(rbuf[:, f, :]), axis=0))
        for bit in (64, 32, 16, 1):
            t = jnp.where((cshift // bit) % 2 == 1, pltpu.roll(t, 128 - bit, 1), t)
        there = t > ABSENT / 2
        if f == 0:
            gap = jnp.where(there, 0.0, -3e38)
            for g in range(8):
                pen[g] = gap[:, 2 * g:2 * g + 1]
        t = jnp.where(there & kept, t, 0.0)
        high = t.astype(BF16).astype(F32)
        near.append(high + pltpu.roll(t - high, 16, 1))
    arounds = []
    for f in range(8):
        around = pltpu.roll(near[f], 32, 1)
        if f > 0:
            around = around + near[f - 1]
        if f < 7:
            around = around + pltpu.roll(near[f + 1], 64, 1)
        arounds.append(around.astype(BF16))
    around = jnp.concatenate(arounds, axis=0)
    out = jnp.maximum(dot(jnp.concatenate([around, around], axis=1), w1[...]), 0.0)
    for at, part in zip((0, 128), halves(out)):
        part = part.reshape(8, 128, 512)
        for p in range(4):
            x1[p, 1:9, :, at:at + 128] = part[:, :, p * 128:(p + 1) * 128]

    for p in range(4):
        out = dot(jnp.concatenate([x1[p, i:i + 8].reshape(1024, 256) for i in range(3)], axis=1), w2[...])
        out = jnp.maximum(out[:, :128] + out[:, 128:], 0.0)
        row = [out[f * 128:(f + 1) * 128] for f in range(8)]
        for pair in range(4):
            d1, d2 = row[2 * pair], row[2 * pair + 1]
            mixes = (
                row[2 * pair - 1] - d2 if pair else -d2, d1 + d2, d2 - d1,
                d1 - row[2 * pair + 2] if pair < 3 else d1,
            )
            for j, mix in enumerate(mixes):
                for ref, part in zip((x2h, x2l), halves(mix)):
                    at = j * 4 + pair
                    ref[p + 1, at, :, 0:128] = part
                    ref[p, at, :, 128:192] = part[:, 0:64]
                    ref[p + 2, at, :, 192:256] = part[:, 64:128]

    scale = jnp.concatenate([out_v[...], out_v[...]], axis=1)
    best = [None, None]

    for p in range(4):
        for j in range(4):
            upper = x2h[p + 1, j * 4:j * 4 + 4].reshape(512, 256)
            lower = x2l[p + 1, j * 4:j * 4 + 4].reshape(512, 256)
            products[p % 2, j] = dot(jnp.concatenate([upper, lower, upper], axis=1), w3[j * 768:(j + 1) * 768, :])
        m0, m1, m2, m3 = (products[p % 2, j] for j in range(4))
        for at, out in enumerate((m0 + m1 + m2, m1 - m2 - m3)):
            out = jnp.maximum(out, 0.0) * scale
            for s in range(2):
                total = jnp.sum(out[:, s * 128:(s + 1) * 128], axis=1, keepdims=True)
                total = total.reshape(4, 128, 1) + pen[2 * p + s][None]
                best[at] = total if best[at] is None else jnp.maximum(best[at], total)
    mean = jnp.sum(best[0] + best[1], axis=0) * 0.125
    refined_ref[...] = jnp.sum(
        jnp.where(iota((128, 128), 0) == iota((128, 128), 1), mean, 0.0), axis=0, keepdims=True
    )

    for name, block in (("b", b_r), ("c1", b_q), ("c3", b_s)):
        wait(("coarse", name), cbuf.at[block])
    n, col = iota((128, 256), 0), iota((128, 256), 1)
    ny = (n // 2) % 4
    nxh, nb = (n // 8) % 2, ((ny + 1) // 2) % 2
    want = (nxh * 2 + nb) * 64 + (n // 16) * 8 + (ny // 2) * 2 + n % 2
    scores = pick(jnp.where(col == want, 1.0, 0.0).astype(BF16), cbuf[...].reshape(256, 128))
    relation = (nxh != xh).astype(jnp.int32)[:, :128] + 2 * (nb != b).astype(jnp.int32)[:, :128]
    mine = scores
    for r in range(1, 4):
        mine = jnp.where(relation == r, pltpu.roll(scores, 128 - 32 * r, 1), mine)
    coarse_ref[...] = mine.T[0:4]

    for sent in started:
        sent.wait_send()

    def sent_wait(t, _):
        msg_copy(t // 4, (t // 2) % 2, t % 2).wait_send()
        return 0

    lax.fori_loop(1, 32, sent_wait, 0)


def local(queries, database, db_frames, cand_shard, cand_local, conv_one, conv_two, conv_three, conv_out):
    anywhere = pl.BlockSpec(memory_space=pltpu.HBM)
    vmem = pl.BlockSpec(memory_space=pltpu.VMEM)
    smem = pl.BlockSpec(memory_space=pltpu.SMEM)
    coarse, refined = pl.pallas_call(
        kernel,
        out_shape=(jax.ShapeDtypeStruct((4, 128), F32), jax.ShapeDtypeStruct((1, 128), F32)),
        in_specs=[anywhere, anywhere, smem] + [anywhere] * 6,
        out_specs=(vmem, vmem),
        scratch_shapes=[
            pltpu.VMEM((32, 128, K), BF16),
            pltpu.VMEM((16, 128, K), BF16),
            pltpu.VMEM((4, 2, 256, K), BF16),
            pltpu.VMEM((32, 8, 128), F32),
            pltpu.VMEM((4, 8, 128), F32),
            pltpu.VMEM((32, 8, 128), F32),
            pltpu.VMEM((32, 8, 128), F32),
            pltpu.VMEM((4, 8, 8, 128), F32),
            pltpu.VMEM((256, 256), BF16),
            pltpu.VMEM((1, 128), jnp.int32),
            pltpu.VMEM((1, 128), jnp.int32),
            pltpu.VMEM((3, 3, 1, 32), F32),
            pltpu.VMEM((288, 64), F32),
            pltpu.VMEM((576, 128), F32),
            pltpu.VMEM((1, 128), F32),
            pltpu.VMEM((256, 512), BF16),
            pltpu.VMEM((768, 256), BF16),
            pltpu.VMEM((3072, 256), BF16),
            pltpu.VMEM((4, 10, 128, 256), BF16),
            pltpu.VMEM((6, 16, 128, 256), BF16),
            pltpu.VMEM((6, 16, 128, 256), BF16),
            pltpu.VMEM((2, 4, 512, 256), F32),
            pltpu.VMEM((8, 128, 1), F32),
            pltpu.SemaphoreType.DMA((72,)),
            pltpu.SemaphoreType.DMA((72,)),
            pltpu.SemaphoreType.DMA((32,)),
            pltpu.SemaphoreType.DMA((32,)),
            pltpu.SemaphoreType.DMA((8,)),
        ],
        compiler_params=pltpu.CompilerParams(
            collective_id=0, has_side_effects=True, vmem_limit_bytes=64 * 1024 * 1024
        ),
        cost_estimate=pl.CostEstimate(flops=13_000_000_000, bytes_accessed=2_000_000, transcendentals=0),
    )(
        queries.reshape(128, K), database.reshape(4, 128, K), db_frames, cand_shard.reshape(1, 128),
        cand_local.reshape(1, 128), conv_one, conv_two.reshape(288, 64),
        conv_three.reshape(576, 128), conv_out.reshape(1, 128),
    )
    return coarse.T[None], refined[None]


def solution(mesh):
    in_specs = (
        P("index", "rep", None, None, None),
        P("index", None, None, None),
        P("index"),
        P("index", "rep", None, None),
        P("index", "rep", None),
        P(),
        P(),
        P(),
        P(),
    )
    out_specs = (P("rep", None, "index"), P("index", "rep", None))
    return jax.shard_map(local, mesh=mesh, in_specs=in_specs, out_specs=out_specs, check_vma=False)
```

```python
import functools

import jax
import jax.numpy as jnp
from jax import lax
from jax.experimental import pallas as pl
from jax.experimental.pallas import tpu as pltpu
from jax.sharding import PartitionSpec as P

MESH = pl.DeviceIdType.MESH
F32, BF16 = jnp.float32, jnp.bfloat16
ABSENT = -(2.0 ** 100)
K = 512
ORDER = (
    ("permute", 0), ("permute", 1), ("prepare", 0), ("prepare", 1), ("prepare", 2), ("prepare", 3), ("prepare", 4),
    ("get", "d", (0, 0)), ("prepare", 5), ("prepare", 6), ("prepare", 7), ("prepare", 8), ("prepare", 9),
    ("prepare", 10), ("prepare", 11), ("prepare", 12), ("get", "a", 0), ("put", "+", (1, 2)), ("put", "-", (1, 2)),
    ("get", "+", (1, 1)), ("put", "+", (2, 1)), ("put", "a", 2), ("get", "-", (1, 1)), ("put", "-", (2, 1)),
    ("put", "a", 3), ("get", "a", 1), ("put", "d", (0, 1)), ("get", "+", (1, 0)), ("put", "+", (2, 0)),
    ("put", "d", (1, 0)), ("get", "-", (1, 0)), ("put", "-", (2, 0)), ("put", "d", (2, 0)), ("get", "xh", 0),
    ("put", "xl", 0), ("get", "b", 0), ("put", "xh", 4), ("put", "b", 4), ("put", "xl", 1), ("permute", 2),
    ("get", "d", (0, 1)), ("tile", 0, 0), ("get", "d", (1, 0)), ("get", "d", (2, 0)),
    ("get", "+", (1, 2)), ("put", "+", (2, 2)), ("get", "-", (1, 2)), ("put", "-", (2, 2)), ("get", "xh", 1),
    ("get", "a", 2), ("put", "d", (1, 1)), ("get", "b", 1), ("put", "xh", 5), ("put", "b", 5), ("permute", 3),
    ("tile", 1, 0), ("get", "+", (2, 1)), ("put", "+", (3, 1)), ("put", "a", 4), ("get", "-", (2, 1)),
    ("put", "-", (3, 1)), ("put", "a", 5), ("get", "a", 3), ("put", "d", (2, 1)), ("get", "d", (1, 1)),
    ("tile", 0, 1), ("tile", 1, 1), ("get", "+", (2, 0)), ("put", "+", (3, 0)), ("put", "d", (3, 0)),
    ("get", "-", (2, 0)), ("put", "-", (3, 0)), ("put", "d", (4, 0)), ("get", "d", (2, 1)), ("get", "xl", 0),
    ("tile", 0, 2), ("get", "xh", 4), ("put", "xh", 2), ("get", "b", 4), ("put", "b", 2), ("permute", 4),
    ("get", "d", (3, 0)), ("get", "+", (2, 2)), ("put", "+", (3, 2)), ("get", "-", (2, 2)), ("put", "-", (3, 2)),
    ("get", "d", (4, 0)), ("tile", 1, 2), ("get", "+", (3, 1)), ("put", "+", (4, 1)), ("put", "a", 6),
    ("get", "a", 4), ("put", "d", (3, 1)), ("get", "-", (3, 1)), ("put", "g", 1), ("put", "a", 7), ("get", "xl", 1),
    ("get", "xh", 5), ("get", "b", 5), ("permute", 5), ("permute", 6), ("tile", 2, 2), ("get", "+", (3, 0)),
    ("put", "+", (4, 0)), ("put", "d", (5, 0)), ("get", "a", 5), ("put", "d", (4, 1)), ("get", "d", (3, 1)),
    ("get", "-", (3, 0)), ("put", "g", 0), ("put", "d", (6, 0)), ("tile", 0, 3), ("tile", 1, 3), ("tile", 2, 3),
    ("get", "+", (3, 2)), ("get", "d", (5, 0)), ("get", "-", (3, 2)), ("get", "d", (4, 1)), ("get", "d", (6, 0)),
    ("tile", 0, 4), ("get", "xh", 2), ("get", "b", 2), ("permute", 7), ("get", "a", 6), ("put", "d", (5, 1)),
    ("get", "+", (4, 1)), ("tile", 1, 4), ("tile", 2, 4), ("tile", 3, 4), ("lengths",), ("post", 4), ("get", "g", 1),
    ("get", "d", (5, 1)), ("get", "+", (4, 0)), ("put", "d", (7, 0)), ("tile", 0, 5), ("tile", 1, 5), ("tile", 2, 5),
    ("tile", 3, 5), ("get", "a", 7), ("put", "d", (6, 1)), ("get", "d", (7, 0)), ("get", "g", 0),
    ("put", "d", (7, 1)), ("post", 5), ("tile", 3, 3), ("post", 3), ("tile", 3, 2), ("post", 2), ("get", "d", (6, 1)),
    ("tile", 0, 6), ("get", "d", (7, 1)), ("tile", 0, 7), ("tile", 1, 7), ("tile", 2, 7), ("tile", 3, 7), ("post", 7),
    ("tile", 1, 6), ("tile", 2, 6), ("tile", 3, 6), ("post", 6), ("tile", 2, 1), ("tile", 3, 1), ("post", 1),
    ("tile", 2, 0), ("tile", 3, 0), ("post", 0),
)


def dot(a, b):
    return jnp.dot(a, b, preferred_element_type=F32)


def iota(shape, axis):
    return lax.broadcasted_iota(jnp.int32, shape, axis)


def halves(x):
    high = x.astype(BF16)
    return high, (x - high.astype(F32)).astype(BF16)


def thirds(x):
    high, rest = x.astype(BF16), None
    rest = x - high.astype(F32)
    mid = rest.astype(BF16)
    return high, mid, (rest - mid.astype(F32)).astype(BF16)


def pick(onehot, x):
    y = dot(onehot, jnp.concatenate(thirds(x), axis=1))
    n = x.shape[1]
    return y[:, :n] + (y[:, n:2 * n] + y[:, 2 * n:])


def kernel(
    q_hbm, db_hbm, frames, shard_hbm, local_hbm, one_hbm, two_hbm, three_hbm, out_hbm,
    out_ref,
    qbuf, dbraw, dbp, fmap, lens, msg, rbuf, cbuf, perm,
    shard_v, local_v, one_v, two_v, three_v, out_v,
    w1, w2, w3, x1, x2h, x2l, products, pen,
    send_sem, recv_sem, msg_send, msg_recv, local_sem,
):
    index, rep = lax.axis_index("index"), lax.axis_index("rep")
    c, y, xh, z = index % 2, (index // 2) % 4, (index // 8) % 2, index // 16
    x = xh * 2 + rep
    a, b = y // 2, ((y + 1) // 2) % 2
    ell = rep

    def device(z, x, y, c):
        return (((z * 2 + x // 2) * 4 + y) * 2 + c, x % 2)

    def y_of(a, b):
        return a * 3 + b * (1 - 2 * a)

    me_q = z * 4 + a * 2 + c
    me_b = xh * 2 + b
    b_own, b_q, b_r, b_s = me_b, (1 - xh) * 2 + b, xh * 2 + (1 - b), (1 - xh) * 2 + (1 - b)
    dev = {
        "+": device((z + 1) % 8, x, y, c),
        "-": device((z + 7) % 8, x, y, c),
        "a": device(z, x, 3 - y, c),
        "b": device(z, x, y_of(a, 1 - b), c),
        "d": device(z, x, y, 1 - c),
        "xh": device(z, 3 - x, y, c),
        "xl": device(z, xh * 2 + (1 - rep), y, c),
    }
    far = {
        "c1": device(z, (1 - xh) * 2 + rep, y, c),
        "c3": device(z, (1 - xh) * 2 + rep, y_of(a, 1 - b), c),
    }

    diagonal = device((z + 7) % 8, x, 3 - y, c)

    def row_device(k, da, dc):
        zk, ak, ck = z_at(k), 1 - a if da else a, 1 - c if dc else c
        return zk, ak, ck, device(zk, x, y_of(ak, b), ck)

    barrier = pltpu.get_barrier_semaphore()
    for target in dev.values():
        pl.semaphore_signal(barrier, inc=1, device_id=target, device_id_type=MESH)

    loads = [
        pltpu.make_async_copy(src, dst, local_sem.at[i])
        for i, (src, dst) in enumerate((
            (q_hbm, qbuf.at[me_q]),
            (db_hbm, dbraw.at[pl.ds(me_b * 4, 4)]),
            (three_hbm, three_v),
            (two_hbm, two_v),
            (one_hbm, one_v),
            (shard_hbm, shard_v),
            (local_hbm, local_v),
            (out_hbm, out_v),
        ))
    ]
    for load in loads:
        load.start()

    row8 = iota((8, 128), 0)
    own_lens = jnp.zeros((8, 128), F32)
    for u in range(4):
        own_lens = jnp.where(row8 == u, frames[u].astype(F32), own_lens)
    lens[me_b] = own_lens

    ids, started = {}, []

    def copy(name, src, dst, target):
        sem = ids.setdefault(name, len(ids))
        return pltpu.make_async_remote_copy(
            src_ref=src, dst_ref=dst, send_sem=send_sem.at[sem], recv_sem=recv_sem.at[sem],
            device_id=target, device_id_type=MESH,
        )

    def send(name, src, dst, target):
        started.append(copy(name, src, dst, target))
        started[-1].start()

    def wait(name, dst):
        copy(name, dst, dst, dev["d"]).wait_recv()

    around_z = [(z + ((k + 1) // 2) * (1 - 2 * (k % 2)) + 8) % 8 for k in range(9)]

    def z_at(k):
        return around_z[k]

    def half(zz, aa, h):
        return qbuf.at[zz * 4 + aa * 2 + c, pl.ds(h * 64, 64), :]

    def unit(zz, aa, cc):
        return qbuf.at[zz * 4 + aa * 2 + cc]

    def db_unit(block, u):
        return dbraw.at[block * 4 + u]

    pl.semaphore_wait(barrier, len(dev))

    def ring_send(way, d, item):
        k = 2 * (d - 1) - (1 if way == "+" else 0) if d > 1 else 0
        zz = z_at(k)
        ref = half(zz, 1 - a, 0) if item == 2 else half(zz, a, item)
        src = q_hbm.at[pl.ds(item * 64, 64), :] if d == 1 and item < 2 else ref
        send((way, d, item), src, ref, dev[way])

    def ring_wait(way, d, item):
        zz = z_at(2 * d - (1 if way == "+" else 0))
        wait((way, d, item), half(zz, 1 - a, 0) if item == 2 else half(zz, a, item))

    def db_at(link, position):
        first = {"xh": (2, 3, 1, None, 0, 1), "b": (2, 3, 1, None, 2, 3)}[link]
        block = b_s if position > 3 else b_q if link == "xh" else b_r
        return block, (2 * ell + first[position]) % 4

    def put(link, key):
        name = (link, key)
        if link in "+-":
            ring_send(link, *key)
        elif link == "a":
            if key < 2:
                send(name, q_hbm.at[pl.ds(key * 64, 64), :], half(z, a, key), dev["a"])
            else:
                ref = half(z_at(key - 1), a, 1)
                send(name, ref, ref, dev["a"])
        elif link == "d":
            k, other = key
            ref = unit(z_at(k), 1 - a if other else a, c)
            send(name, ref if k or other else q_hbm, ref, dev["d"])
        elif link == "g":
            ref = half(z_at(6), a, key)
            send(name, ref, ref, diagonal)
        elif link == "xl":
            ref = db_unit(b_r if key else b_q, (2 * ell + 2) % 4)
            send(name, ref, ref, dev["xl"])
        elif key > 3:
            ref = db_unit(b_r if link == "xh" else b_q, (2 * ell + key - 2) % 4)
            send(name, ref, ref, dev[link])
        else:
            first = (0, 1, 3) if link == "xh" else (2, 3, 1)
            u = (2 * ell + first[key]) % 4
            send(name, db_hbm.at[u], db_unit(me_b, u), dev[link])

    def get(link, key):
        name = (link, key)
        if link in "+-":
            ring_wait(link, *key)
        elif link == "a":
            wait(name, half(z, 1 - a, key) if key < 2 else half(z_at(key - 1), 1 - a, 1))
        elif link == "d":
            wait(name, unit(z_at(key[0]), 1 - a if key[1] else a, 1 - c))
        elif link == "g":
            wait(name, half(z_at(7), 1 - a, key))
        elif link == "xl":
            wait(name, db_unit(b_r if key else b_q, 2 * ell))
        else:
            wait(name, db_unit(*db_at(link, key)))

    for link, keys in (
        ("+", ((1, 1),)), ("-", ((1, 1),)), ("a", (0,)), ("+", ((1, 0),)), ("-", ((1, 0),)), ("a", (1,)),
        ("xh", (0,)), ("b", (0,)), ("d", ((0, 0),)), ("xh", (1,)), ("b", (1,)),
    ):
        for key in keys:
            put(link, key)
    send(("len", "b"), lens.at[me_b], lens.at[me_b], dev["b"])

    ri, ci = iota((256, 256), 0), iota((256, 256), 1)
    perm[...] = jnp.where(
        ci == (ri % 2) * 128 + ((ri // 2) % 8) * 16 + ri // 16, 1.0, 0.0
    ).astype(BF16)

    def permute(hb):
        videos = (
            ((b_own, 0), (b_own, 1)), ((b_own, 2), (b_own, 3)),
            (db_at("xh", 0), db_at("b", 0)), (db_at("xh", 1), db_at("b", 1)), (db_at("xh", 4), db_at("b", 4)),
            (db_at("xh", 5), db_at("b", 5)), ((b_q, 2 * ell), (b_r, 2 * ell)), (db_at("xh", 2), db_at("b", 2)),
        )[hb]
        raw = jnp.concatenate([dbraw[block * 4 + u] for block, u in videos], axis=0)
        rows = dot(perm[...], raw).astype(BF16)
        for u in range(16):
            at = (u % 8) * 32 + (hb % 2) * 16
            dbp[hb // 2, u // 8, at:at + 16, :] = rows[u * 16:(u + 1) * 16]

    lane = iota((8, 128), 1)

    def tile(group, k):
        zz = z_at(k)
        left = qbuf[pl.ds(zz * 4, 4)].reshape(512, K)
        top = None
        for t in range(2):
            sim = lax.dot_general(left, dbp[group, t], (((1,), (1,)), ((), ())), preferred_element_type=F32)
            sim = jnp.maximum(sim[:, :128], sim[:, 128:])
            top = sim if top is None else jnp.maximum(top, sim)
        top = jnp.maximum(top, pltpu.roll(top, 64, 1))
        top = jnp.maximum(top, pltpu.roll(top, 32, 1))
        mean = jnp.sum(top.reshape(32, 16, 128), axis=1).reshape(4, 8, 128)
        fmap[group, pl.ds(zz * 4, 4)] = mean

    order = {
        "own": ((0, 0), (0, 1), (1, 0), (1, 1)),
        "q": ((6, 0), (7, 0), (2, 0), (3, 0)),
        "r": ((6, 1), (7, 1), (2, 1), (3, 1)),
        "s": ((4, 0), (5, 0), (4, 1), (5, 1)),
    }
    blocks = {"own": b_own, "q": b_q, "r": b_r, "s": b_s}

    def unit_of(name, i):
        return i if name == "own" else (2 * ell + i) % 4

    def length_lanes():
        total = jnp.zeros((1, 128), F32)
        lane1 = iota((1, 128), 1)
        for name, places in order.items():
            for i, (hb, v) in enumerate(places):
                value = lens[blocks[name], pl.ds(unit_of(name, i), 1), :]
                total = jnp.where((lane1 // 16 == hb) & (lane1 % 2 == v), value, total)
        return (lane1 % 16 // 2).astype(F32) < total

    def post(k):
        zz = z_at(k)
        rows = jnp.zeros((8, 128), F32)
        for i in range(4):
            maps = fmap[0, zz * 4 + i]
            for group in range(1, 4):
                maps = jnp.where(lane // 32 == group, fmap[group, zz * 4 + i], maps)
            maps = maps * (K ** -0.5 / 16)
            maps = jnp.where(present, maps, ABSENT)
            msg[zz * 4 + i] = maps
            for shift in (8, 4, 2):
                maps = jnp.maximum(maps, pltpu.roll(maps, 128 - shift, 1))
            rows = jnp.where(row8 == i, jnp.sum(maps, axis=0, keepdims=True), rows)
        cbuf[me_b, zz] = rows
        for da in range(2):
            for dc in range(2):
                zk, ak, ck, target = row_device(k, da, dc)
                slot = zk * 4 + ak * 2 + ck
                if k == 0 and da == 0 and dc == 0:
                    rbuf[me_q] = msg[slot]
                else:
                    pltpu.make_async_remote_copy(
                        src_ref=msg.at[slot], dst_ref=rbuf.at[me_q], send_sem=msg_send.at[0],
                        recv_sem=msg_recv.at[0], device_id=target, device_id_type=MESH,
                    ).start()

    def third_weights(j):
        zero = jnp.zeros((64, 128), F32)
        taps = [[three_v[(i * 3 + t) * 64:(i * 3 + t + 1) * 64, :] for i in range(3)] for t in range(3)]
        w = []
        for g0, g1, g2 in taps:
            w.append((g0, (g0 + g2 + g1) * 0.5, (g0 + g2 - g1) * 0.5, g2)[j])
        for r, (left, right) in enumerate(((w[1], w[0]), (w[2], w[1]), (zero, w[2]), (w[0], zero))):
            for s, part in enumerate((left, right)):
                high, low = halves(part)
                for at, value in ((0, high), (256, high), (512, low)):
                    at = j * 768 + at + r * 64
                    w3[at:at + 64, s * 128:(s + 1) * 128] = value

    def second_weights(i):
        place = [jnp.where(iota((64, 128), 1) == iota((64, 128), 0) + 64 * s, 1.0, 0.0).astype(BF16) for s in range(2)]
        zero = jnp.zeros((32, 64), F32)
        w = [two_v[(i * 3 + j) * 32:(i * 3 + j + 1) * 32, :] for j in range(3)]
        stacks = (jnp.concatenate(w + [zero], axis=0), jnp.concatenate([zero] + w, axis=0))
        for part in range(2):
            value = sum(dot(halves(stack)[part], where) for stack, where in zip(stacks, place)).astype(BF16)
            for r in range(2):
                w2[i * 256 + r * 128:i * 256 + (r + 1) * 128, part * 128:(part + 1) * 128] = value

    def first_weights(i):
        spread = jnp.where(iota((32, 512), 1) % 32 == iota((32, 512), 0), 1.0, 0.0).astype(BF16)
        j, col = iota((32, 512), 0), iota((32, 512), 1)
        g = (j % 16) // 2
        pos = 2 * (col // 128) - 1 + (col % 128) // 32
        for part in range(2):
            value = jnp.zeros((32, 512), F32)
            for s in range(3):
                line = dot(halves(jnp.broadcast_to(one_v[i, s], (16, 32)))[part], spread)[0:1]
                hit = (g - pos + 1 == s) & (pos >= 0) & (pos < 8) & (j % 2 == 0)
                value = value + jnp.where(hit, line, 0.0)
            w1[part * 128 + i * 32:part * 128 + (i + 1) * 32, :] = value.astype(BF16)
            if i == 0:
                w1[part * 128 + 96:part * 128 + 128, :] = jnp.zeros((32, 512), BF16)

    def clear_ends(ref):
        for p in range(4):
            for f in (0, 9):
                ref[p, f] = jnp.zeros((128, 256), BF16)

    def clear_sides(ref):
        for p in (1, 4):
            ref[p, :, :, 128:256] = jnp.zeros((16, 128, 128), BF16)

    def prepare(i):
        if i == 0:
            for load in (2, 3, 4):
                loads[load].wait()
        (
            *[functools.partial(third_weights, t) for t in range(4)],
            *[functools.partial(second_weights, t) for t in range(3)],
            *[functools.partial(first_weights, t) for t in range(3)],
            functools.partial(clear_ends, x1),
            *[functools.partial(clear_sides, ref) for ref in (x2h, x2l)],
        )[i]()

    present = None
    loads[0].wait()
    loads[1].wait()
    for step, *which in ORDER:
        if step == "lengths":
            for name, block in (("b", b_r), ("c1", b_q), ("c3", b_s)):
                wait(("len", name), lens.at[block])
            present = length_lanes()
        else:
            dict(get=get, put=put, permute=permute, tile=tile, post=post, prepare=prepare)[step](*which)
        if (step, *which) == ("get", "xh", 4):
            for name in ("c1", "c3"):
                send(("len", name), lens.at[me_b], lens.at[me_b], far[name])
    ri, ci = iota((128, 128), 0), iota((128, 128), 1)
    where = ri < 0
    for r, (name, places) in enumerate(order.items()):
        for i, (hb, v) in enumerate(places):
            where = where | ((ri == hb * 16 + v) & (ci == r * 32 + unit_of(name, i)))
    sums = cbuf[me_b].reshape(64, 128)
    where = jnp.where(where, 1.0, 0.0).astype(BF16)
    sums = sum(dot(part, where) for part in thirds(sums)) * 0.125
    cbuf[me_b] = sums.reshape(8, 8, 128)
    for name in ("b", "c1", "c3"):
        send(("coarse", name), cbuf.at[me_b], cbuf.at[me_b], (dev | far)[name])

    def column(row):
        return jnp.sum(
            jnp.where(iota((128, 128), 0) == iota((128, 128), 1), row.astype(F32), 0.0), axis=1, keepdims=True
        ).astype(jnp.int32)

    for i in (5, 6, 7):
        loads[i].wait()
    shard, place = column(shard_v[...]), column(local_v[...])
    cy = (shard // 2) % 4
    ca, cb = cy // 2, ((cy + 1) // 2) % 2
    source = (shard // 16) * 4 + ca * 2 + shard % 2
    cross, other = ((shard // 8) % 2) != xh, cb != b
    offset = (place + 2 * ell) % 4
    chb, cv = place // 2, place % 2
    for rule, name in ((cross & ~other, "q"), (other & ~cross, "r"), (cross & other, "s")):
        for i, (hb, v) in enumerate(order[name]):
            hit = rule & (offset == i)
            chb, cv = jnp.where(hit, hb, chb), jnp.where(hit, v, cv)
    cshift = chb * 16 + cv
    cols = iota((128, 96), 1)
    onehot = jnp.where(cols % 32 == source, 1.0, 0.0).astype(BF16)

    for sent in started:
        sent.wait_send()
    messages = pltpu.make_async_remote_copy(
        src_ref=msg.at[pl.ds(0, 31)], dst_ref=rbuf.at[pl.ds(0, 31)], send_sem=msg_send.at[0],
        recv_sem=msg_recv.at[0], device_id=dev["d"], device_id_type=MESH,
    )
    messages.wait_send()
    messages.wait_recv()
    lane = iota((128, 128), 1)
    kept = (lane < 16) & (lane % 2 == 0)
    near = []
    for f in range(8):
        t = dot(onehot, jnp.concatenate(thirds(rbuf[:, f, :]), axis=0))
        for bit in (64, 32, 16, 1):
            t = jnp.where((cshift // bit) % 2 == 1, pltpu.roll(t, 128 - bit, 1), t)
        there = t > ABSENT / 2
        if f == 0:
            gap = jnp.where(there, 0.0, -3e38)
            for g in range(8):
                pen[g] = gap[:, 2 * g:2 * g + 1]
        t = jnp.where(there & kept, t, 0.0)
        high = t.astype(BF16).astype(F32)
        near.append(high + pltpu.roll(t - high, 16, 1))
    arounds = []
    for f in range(8):
        around = pltpu.roll(near[f], 32, 1)
        if f > 0:
            around = around + near[f - 1]
        if f < 7:
            around = around + pltpu.roll(near[f + 1], 64, 1)
        arounds.append(around.astype(BF16))
    around = jnp.concatenate(arounds, axis=0)
    out = jnp.maximum(dot(jnp.concatenate([around, around], axis=1), w1[...]), 0.0)
    for at, part in zip((0, 128), halves(out)):
        part = part.reshape(8, 128, 512)
        for p in range(4):
            x1[p, 1:9, :, at:at + 128] = part[:, :, p * 128:(p + 1) * 128]

    for p in range(4):
        out = dot(jnp.concatenate([x1[p, i:i + 8].reshape(1024, 256) for i in range(3)], axis=1), w2[...])
        out = jnp.maximum(out[:, :128] + out[:, 128:], 0.0)
        row = [out[f * 128:(f + 1) * 128] for f in range(8)]
        for pair in range(4):
            d1, d2 = row[2 * pair], row[2 * pair + 1]
            mixes = (
                row[2 * pair - 1] - d2 if pair else -d2, d1 + d2, d2 - d1,
                d1 - row[2 * pair + 2] if pair < 3 else d1,
            )
            for j, mix in enumerate(mixes):
                for ref, part in zip((x2h, x2l), halves(mix)):
                    at = j * 4 + pair
                    ref[p + 1, at, :, 0:128] = part
                    ref[p, at, :, 128:192] = part[:, 0:64]
                    ref[p + 2, at, :, 192:256] = part[:, 64:128]

    scale = jnp.concatenate([out_v[...], out_v[...]], axis=1)
    best = [None, None]

    for p in range(4):
        for j in range(4):
            upper = x2h[p + 1, j * 4:j * 4 + 4].reshape(512, 256)
            lower = x2l[p + 1, j * 4:j * 4 + 4].reshape(512, 256)
            products[p % 2, j] = dot(jnp.concatenate([upper, lower, upper], axis=1), w3[j * 768:(j + 1) * 768, :])
        m0, m1, m2, m3 = (products[p % 2, j] for j in range(4))
        for at, out in enumerate((m0 + m1 + m2, m1 - m2 - m3)):
            out = jnp.maximum(out, 0.0) * scale
            for s in range(2):
                total = jnp.sum(out[:, s * 128:(s + 1) * 128], axis=1, keepdims=True)
                total = total.reshape(4, 128, 1) + pen[2 * p + s][None]
                best[at] = total if best[at] is None else jnp.maximum(best[at], total)
    mean = jnp.sum(best[0] + best[1], axis=0) * 0.125
    out_ref[4:5, :] = jnp.sum(
        jnp.where(iota((128, 128), 0) == iota((128, 128), 1), mean, 0.0), axis=0, keepdims=True
    )

    for name, block in (("b", b_r), ("c1", b_q), ("c3", b_s)):
        wait(("coarse", name), cbuf.at[block])
    n, col = iota((128, 256), 0), iota((128, 256), 1)
    ny = (n // 2) % 4
    nxh, nb = (n // 8) % 2, ((ny + 1) // 2) % 2
    want = (nxh * 2 + nb) * 64 + (n // 16) * 8 + (ny // 2) * 2 + n % 2
    scores = pick(jnp.where(col == want, 1.0, 0.0).astype(BF16), cbuf[...].reshape(256, 128))
    relation = (nxh != xh).astype(jnp.int32)[:, :128] + 2 * (nb != b).astype(jnp.int32)[:, :128]
    mine = scores
    for r in range(1, 4):
        mine = jnp.where(relation == r, pltpu.roll(scores, 128 - 32 * r, 1), mine)
    out_ref[0:4, :] = mine.T[0:4]


def split_rows(scores_ref, coarse_ref, refined_ref):
    coarse_ref[...] = scores_ref[0:4, :]
    refined_ref[...] = scores_ref[4:5, :]


def local(queries, database, db_frames, cand_shard, cand_local, conv_one, conv_two, conv_three, conv_out):
    anywhere = pl.BlockSpec(memory_space=pltpu.HBM)
    vmem = pl.BlockSpec(memory_space=pltpu.VMEM)
    smem = pl.BlockSpec(memory_space=pltpu.SMEM)
    scores = pl.pallas_call(
        kernel,
        out_shape=jax.ShapeDtypeStruct((8, 128), F32),
        in_specs=[anywhere, anywhere, smem] + [anywhere] * 6,
        out_specs=vmem,
        scratch_shapes=[
            pltpu.VMEM((32, 128, K), BF16),
            pltpu.VMEM((16, 128, K), BF16),
            pltpu.VMEM((4, 2, 256, K), BF16),
            pltpu.VMEM((4, 32, 8, 128), F32),
            pltpu.VMEM((4, 8, 128), F32),
            pltpu.VMEM((32, 8, 128), F32),
            pltpu.VMEM((32, 8, 128), F32),
            pltpu.VMEM((4, 8, 8, 128), F32),
            pltpu.VMEM((256, 256), BF16),
            pltpu.VMEM((1, 128), jnp.int32),
            pltpu.VMEM((1, 128), jnp.int32),
            pltpu.VMEM((3, 3, 1, 32), F32),
            pltpu.VMEM((288, 64), F32),
            pltpu.VMEM((576, 128), F32),
            pltpu.VMEM((1, 128), F32),
            pltpu.VMEM((256, 512), BF16),
            pltpu.VMEM((768, 256), BF16),
            pltpu.VMEM((3072, 256), BF16),
            pltpu.VMEM((4, 10, 128, 256), BF16),
            pltpu.VMEM((6, 16, 128, 256), BF16),
            pltpu.VMEM((6, 16, 128, 256), BF16),
            pltpu.VMEM((2, 4, 512, 256), F32),
            pltpu.VMEM((8, 128, 1), F32),
            pltpu.SemaphoreType.DMA((72,)),
            pltpu.SemaphoreType.DMA((72,)),
            pltpu.SemaphoreType.DMA((1,)),
            pltpu.SemaphoreType.DMA((1,)),
            pltpu.SemaphoreType.DMA((8,)),
        ],
        compiler_params=pltpu.CompilerParams(
            collective_id=0, has_side_effects=True, vmem_limit_bytes=64 * 1024 * 1024
        ),
        cost_estimate=pl.CostEstimate(flops=13_000_000_000, bytes_accessed=2_000_000, transcendentals=0),
    )(
        queries.reshape(128, K), database.reshape(4, 128, K), db_frames, cand_shard.reshape(1, 128),
        cand_local.reshape(1, 128), conv_one, conv_two.reshape(288, 64),
        conv_three.reshape(576, 128), conv_out.reshape(1, 128),
    )
    coarse, refined = pl.pallas_call(
        split_rows,
        out_shape=(jax.ShapeDtypeStruct((4, 128), F32), jax.ShapeDtypeStruct((1, 128), F32)),
    )(scores)
    return coarse.T[None], refined[None]


def solution(mesh):
    in_specs = (
        P("index", "rep", None, None, None),
        P("index", None, None, None),
        P("index"),
        P("index", "rep", None, None),
        P("index", "rep", None),
        P(),
        P(),
        P(),
        P(),
    )
    out_specs = (P("rep", None, "index"), P("index", "rep", None))
    return jax.shard_map(local, mesh=mesh, in_specs=in_specs, out_specs=out_specs, check_vma=False)
```

```python
import functools

import jax
import jax.numpy as jnp
from jax import lax
from jax.experimental import pallas as pl
from jax.experimental.pallas import tpu as pltpu
from jax.sharding import PartitionSpec as P

MESH = pl.DeviceIdType.MESH
F32, BF16 = jnp.float32, jnp.bfloat16
ABSENT = -(2.0 ** 100)
K = 512
ORDER = (
    ("permute", 0), ("permute", 1), ("prepare", 0), ("prepare", 1), ("prepare", 2), ("prepare", 3), ("prepare", 4),
    ("get", "d", (0, 0)), ("prepare", 5), ("prepare", 6), ("prepare", 7), ("prepare", 8), ("prepare", 9),
    ("prepare", 10), ("prepare", 11), ("prepare", 12), ("get", "a", 0), ("put", "+", (1, 2)), ("put", "-", (1, 2)),
    ("get", "+", (1, 1)), ("put", "+", (2, 1)), ("put", "a", 2), ("get", "-", (1, 1)), ("put", "-", (2, 1)),
    ("put", "a", 3), ("get", "a", 1), ("put", "d", (0, 1)), ("get", "+", (1, 0)), ("put", "+", (2, 0)),
    ("put", "d", (1, 0)), ("get", "-", (1, 0)), ("put", "-", (2, 0)), ("put", "d", (2, 0)), ("get", "xh", 0),
    ("put", "xl", 0), ("get", "b", 0), ("put", "xh", 4), ("put", "b", 4), ("put", "xl", 1), ("permute", 2),
    ("get", "d", (0, 1)), ("tile", 0, 0), ("get", "d", (1, 0)), ("get", "d", (2, 0)),
    ("get", "+", (1, 2)), ("put", "+", (2, 2)), ("get", "-", (1, 2)), ("put", "-", (2, 2)), ("get", "xh", 1),
    ("get", "a", 2), ("put", "d", (1, 1)), ("get", "b", 1), ("put", "xh", 5), ("put", "b", 5), ("permute", 3),
    ("tile", 1, 0), ("get", "+", (2, 1)), ("put", "+", (3, 1)), ("put", "a", 4), ("get", "-", (2, 1)),
    ("put", "-", (3, 1)), ("put", "a", 5), ("get", "a", 3), ("put", "d", (2, 1)), ("get", "d", (1, 1)),
    ("tile", 0, 1), ("tile", 1, 1), ("get", "+", (2, 0)), ("put", "+", (3, 0)), ("put", "d", (3, 0)),
    ("get", "-", (2, 0)), ("put", "-", (3, 0)), ("put", "d", (4, 0)), ("get", "d", (2, 1)), ("get", "xl", 0),
    ("tile", 0, 2), ("get", "xh", 4), ("put", "xh", 2), ("get", "b", 4), ("put", "b", 2), ("permute", 4),
    ("get", "d", (3, 0)), ("get", "+", (2, 2)), ("put", "+", (3, 2)), ("get", "-", (2, 2)), ("put", "-", (3, 2)),
    ("get", "d", (4, 0)), ("tile", 1, 2), ("get", "+", (3, 1)), ("put", "+", (4, 1)), ("put", "a", 6),
    ("get", "a", 4), ("put", "d", (3, 1)), ("get", "-", (3, 1)), ("put", "g", 1), ("put", "a", 7), ("get", "xl", 1),
    ("get", "xh", 5), ("get", "b", 5), ("permute", 5), ("permute", 6), ("tile", 2, 2), ("get", "+", (3, 0)),
    ("put", "+", (4, 0)), ("put", "d", (5, 0)), ("get", "a", 5), ("put", "d", (4, 1)), ("get", "d", (3, 1)),
    ("get", "-", (3, 0)), ("put", "g", 0), ("put", "d", (6, 0)), ("tile", 0, 3), ("tile", 1, 3), ("tile", 2, 3),
    ("get", "+", (3, 2)), ("get", "d", (5, 0)), ("get", "-", (3, 2)), ("get", "d", (4, 1)), ("get", "d", (6, 0)),
    ("tile", 0, 4), ("get", "xh", 2), ("get", "b", 2), ("permute", 7), ("get", "a", 6), ("put", "d", (5, 1)),
    ("get", "+", (4, 1)), ("tile", 1, 4), ("tile", 2, 4), ("tile", 3, 4), ("lengths",), ("post", 4), ("get", "g", 1),
    ("get", "d", (5, 1)), ("get", "+", (4, 0)), ("put", "d", (7, 0)), ("tile", 0, 5), ("tile", 1, 5), ("tile", 2, 5),
    ("tile", 3, 5), ("get", "a", 7), ("put", "d", (6, 1)), ("get", "d", (7, 0)), ("get", "g", 0),
    ("put", "d", (7, 1)), ("post", 5), ("tile", 3, 3), ("post", 3), ("tile", 3, 2), ("post", 2), ("get", "d", (6, 1)),
    ("tile", 0, 6), ("get", "d", (7, 1)), ("tile", 0, 7), ("tile", 1, 7), ("tile", 2, 7), ("tile", 3, 7), ("post", 7),
    ("tile", 1, 6), ("tile", 2, 6), ("tile", 3, 6), ("post", 6), ("tile", 2, 1), ("tile", 3, 1), ("post", 1),
    ("tile", 2, 0), ("tile", 3, 0), ("post", 0),
)


def dot(a, b):
    return jnp.dot(a, b, preferred_element_type=F32)


def iota(shape, axis):
    return lax.broadcasted_iota(jnp.int32, shape, axis)


def halves(x):
    high = x.astype(BF16)
    return high, (x - high.astype(F32)).astype(BF16)


def thirds(x):
    high, rest = x.astype(BF16), None
    rest = x - high.astype(F32)
    mid = rest.astype(BF16)
    return high, mid, (rest - mid.astype(F32)).astype(BF16)


def pick(onehot, x):
    y = dot(onehot, jnp.concatenate(thirds(x), axis=1))
    n = x.shape[1]
    return y[:, :n] + (y[:, n:2 * n] + y[:, 2 * n:])


def kernel(
    q_hbm, db_hbm, frames, shard_hbm, local_hbm, one_hbm, two_hbm, three_hbm, out_hbm,
    out_ref,
    qbuf, dbraw, dbp, fmap, lens, msg, rbuf, cbuf, perm,
    shard_v, local_v, one_v, two_v, three_v, out_v,
    w1, w2, w3, x1, x2h, x2l, products, pen,
    send_sem, recv_sem, msg_send, msg_recv, local_sem,
):
    index, rep = lax.axis_index("index"), lax.axis_index("rep")
    c, y, xh, z = index % 2, (index // 2) % 4, (index // 8) % 2, index // 16
    x = xh * 2 + rep
    a, b = y // 2, ((y + 1) // 2) % 2
    ell = rep

    def device(z, x, y, c):
        return (((z * 2 + x // 2) * 4 + y) * 2 + c, x % 2)

    def y_of(a, b):
        return a * 3 + b * (1 - 2 * a)

    me_q = z * 4 + a * 2 + c
    me_b = xh * 2 + b
    b_own, b_q, b_r, b_s = me_b, (1 - xh) * 2 + b, xh * 2 + (1 - b), (1 - xh) * 2 + (1 - b)
    dev = {
        "+": device((z + 1) % 8, x, y, c),
        "-": device((z + 7) % 8, x, y, c),
        "a": device(z, x, 3 - y, c),
        "b": device(z, x, y_of(a, 1 - b), c),
        "d": device(z, x, y, 1 - c),
        "xh": device(z, 3 - x, y, c),
        "xl": device(z, xh * 2 + (1 - rep), y, c),
    }
    far = {
        "c1": device(z, (1 - xh) * 2 + rep, y, c),
        "c3": device(z, (1 - xh) * 2 + rep, y_of(a, 1 - b), c),
    }

    diagonal = device((z + 7) % 8, x, 3 - y, c)

    def row_device(k, da, dc):
        zk, ak, ck = z_at(k), 1 - a if da else a, 1 - c if dc else c
        return zk, ak, ck, device(zk, x, y_of(ak, b), ck)

    barrier = pltpu.get_barrier_semaphore()
    for target in dev.values():
        pl.semaphore_signal(barrier, inc=1, device_id=target, device_id_type=MESH)

    loads = [
        pltpu.make_async_copy(src, dst, local_sem.at[i])
        for i, (src, dst) in enumerate((
            (q_hbm, qbuf.at[me_q]),
            (db_hbm, dbraw.at[pl.ds(me_b * 4, 4)]),
            (three_hbm, three_v),
            (two_hbm, two_v),
            (one_hbm, one_v),
            (shard_hbm, shard_v),
            (local_hbm, local_v),
            (out_hbm, out_v),
        ))
    ]
    for load in loads:
        load.start()

    row8 = iota((8, 128), 0)
    own_lens = jnp.zeros((8, 128), F32)
    for u in range(4):
        own_lens = jnp.where(row8 == u, frames[u].astype(F32), own_lens)
    lens[me_b] = own_lens

    ids, started = {}, []

    def copy(name, src, dst, target):
        sem = ids.setdefault(name, len(ids))
        return pltpu.make_async_remote_copy(
            src_ref=src, dst_ref=dst, send_sem=send_sem.at[sem], recv_sem=recv_sem.at[sem],
            device_id=target, device_id_type=MESH,
        )

    def send(name, src, dst, target):
        started.append(copy(name, src, dst, target))
        started[-1].start()

    def wait(name, dst):
        copy(name, dst, dst, dev["d"]).wait_recv()

    around_z = [(z + ((k + 1) // 2) * (1 - 2 * (k % 2)) + 8) % 8 for k in range(9)]

    def z_at(k):
        return around_z[k]

    def half(zz, aa, h):
        return qbuf.at[zz * 4 + aa * 2 + c, pl.ds(h * 64, 64), :]

    def unit(zz, aa, cc):
        return qbuf.at[zz * 4 + aa * 2 + cc]

    def db_unit(block, u):
        return dbraw.at[block * 4 + u]

    pl.semaphore_wait(barrier, len(dev))

    def ring_send(way, d, item):
        k = 2 * (d - 1) - (1 if way == "+" else 0) if d > 1 else 0
        zz = z_at(k)
        ref = half(zz, 1 - a, 0) if item == 2 else half(zz, a, item)
        src = q_hbm.at[pl.ds(item * 64, 64), :] if d == 1 and item < 2 else ref
        send((way, d, item), src, ref, dev[way])

    def ring_wait(way, d, item):
        zz = z_at(2 * d - (1 if way == "+" else 0))
        wait((way, d, item), half(zz, 1 - a, 0) if item == 2 else half(zz, a, item))

    def db_at(link, position):
        first = {"xh": (2, 3, 1, None, 0, 1), "b": (2, 3, 1, None, 2, 3)}[link]
        block = b_s if position > 3 else b_q if link == "xh" else b_r
        return block, (2 * ell + first[position]) % 4

    def put(link, key):
        name = (link, key)
        if link in "+-":
            ring_send(link, *key)
        elif link == "a":
            if key < 2:
                send(name, q_hbm.at[pl.ds(key * 64, 64), :], half(z, a, key), dev["a"])
            else:
                ref = half(z_at(key - 1), a, 1)
                send(name, ref, ref, dev["a"])
        elif link == "d":
            k, other = key
            ref = unit(z_at(k), 1 - a if other else a, c)
            send(name, ref if k or other else q_hbm, ref, dev["d"])
        elif link == "g":
            ref = half(z_at(6), a, key)
            send(name, ref, ref, diagonal)
        elif link == "xl":
            ref = db_unit(b_r if key else b_q, (2 * ell + 2) % 4)
            send(name, ref, ref, dev["xl"])
        elif key > 3:
            ref = db_unit(b_r if link == "xh" else b_q, (2 * ell + key - 2) % 4)
            send(name, ref, ref, dev[link])
        else:
            first = (0, 1, 3) if link == "xh" else (2, 3, 1)
            u = (2 * ell + first[key]) % 4
            send(name, db_hbm.at[u], db_unit(me_b, u), dev[link])

    def get(link, key):
        name = (link, key)
        if link in "+-":
            ring_wait(link, *key)
        elif link == "a":
            wait(name, half(z, 1 - a, key) if key < 2 else half(z_at(key - 1), 1 - a, 1))
        elif link == "d":
            wait(name, unit(z_at(key[0]), 1 - a if key[1] else a, 1 - c))
        elif link == "g":
            wait(name, half(z_at(7), 1 - a, key))
        elif link == "xl":
            wait(name, db_unit(b_r if key else b_q, 2 * ell))
        else:
            wait(name, db_unit(*db_at(link, key)))

    for link, keys in (
        ("+", ((1, 1),)), ("-", ((1, 1),)), ("a", (0,)), ("+", ((1, 0),)), ("-", ((1, 0),)), ("a", (1,)),
        ("xh", (0,)), ("b", (0,)), ("d", ((0, 0),)), ("xh", (1,)), ("b", (1,)),
    ):
        for key in keys:
            put(link, key)
    send(("len", "b"), lens.at[me_b], lens.at[me_b], dev["b"])

    ri, ci = iota((256, 256), 0), iota((256, 256), 1)
    perm[...] = jnp.where(
        ci == (ri % 2) * 128 + ((ri // 2) % 8) * 16 + ri // 16, 1.0, 0.0
    ).astype(BF16)

    def permute(hb):
        videos = (
            ((b_own, 0), (b_own, 1)), ((b_own, 2), (b_own, 3)),
            (db_at("xh", 0), db_at("b", 0)), (db_at("xh", 1), db_at("b", 1)), (db_at("xh", 4), db_at("b", 4)),
            (db_at("xh", 5), db_at("b", 5)), ((b_q, 2 * ell), (b_r, 2 * ell)), (db_at("xh", 2), db_at("b", 2)),
        )[hb]
        raw = jnp.concatenate([dbraw[block * 4 + u] for block, u in videos], axis=0)
        rows = dot(perm[...], raw).astype(BF16)
        for u in range(16):
            at = (u % 8) * 32 + (hb % 2) * 16
            dbp[hb // 2, u // 8, at:at + 16, :] = rows[u * 16:(u + 1) * 16]

    lane = iota((8, 128), 1)

    def tile(group, k):
        zz = z_at(k)
        left = qbuf[pl.ds(zz * 4, 4)].reshape(512, K)
        top = None
        for t in range(2):
            sim = lax.dot_general(left, dbp[group, t], (((1,), (1,)), ((), ())), preferred_element_type=F32)
            sim = jnp.maximum(sim[:, :128], sim[:, 128:])
            top = sim if top is None else jnp.maximum(top, sim)
        top = jnp.maximum(top, pltpu.roll(top, 64, 1))
        top = jnp.maximum(top, pltpu.roll(top, 32, 1))
        mean = jnp.sum(top.reshape(32, 16, 128), axis=1).reshape(4, 8, 128)
        fmap[group, pl.ds(zz * 4, 4)] = mean

    order = {
        "own": ((0, 0), (0, 1), (1, 0), (1, 1)),
        "q": ((6, 0), (7, 0), (2, 0), (3, 0)),
        "r": ((6, 1), (7, 1), (2, 1), (3, 1)),
        "s": ((4, 0), (5, 0), (4, 1), (5, 1)),
    }
    blocks = {"own": b_own, "q": b_q, "r": b_r, "s": b_s}

    def unit_of(name, i):
        return i if name == "own" else (2 * ell + i) % 4

    def length_lanes():
        total = jnp.zeros((1, 128), F32)
        lane1 = iota((1, 128), 1)
        for name, places in order.items():
            for i, (hb, v) in enumerate(places):
                value = lens[blocks[name], pl.ds(unit_of(name, i), 1), :]
                total = jnp.where((lane1 // 16 == hb) & (lane1 % 2 == v), value, total)
        return (lane1 % 16 // 2).astype(F32) < total

    def post(k):
        zz = z_at(k)
        found = []
        for i in range(4):
            maps = fmap[0, zz * 4 + i]
            for group in range(1, 4):
                maps = jnp.where(lane // 32 == group, fmap[group, zz * 4 + i], maps)
            maps = jnp.where(present, maps * (K ** -0.5 / 16), ABSENT)
            msg[zz * 4 + i] = maps
            found.append(maps)
        for da in range(2):
            for dc in range(2):
                zk, ak, ck, target = row_device(k, da, dc)
                slot = zk * 4 + ak * 2 + ck
                if k == 0 and da == 0 and dc == 0:
                    rbuf[me_q] = msg[slot]
                else:
                    pltpu.make_async_remote_copy(
                        src_ref=msg.at[slot], dst_ref=rbuf.at[me_q], send_sem=msg_send.at[0],
                        recv_sem=msg_recv.at[0], device_id=target, device_id_type=MESH,
                    ).start()
        rows = jnp.zeros((8, 128), F32)
        for i, maps in enumerate(found):
            for shift in (8, 4, 2):
                maps = jnp.maximum(maps, pltpu.roll(maps, 128 - shift, 1))
            rows = jnp.where(row8 == i, jnp.sum(maps, axis=0, keepdims=True), rows)
        cbuf[me_b, zz] = rows

    def third_weights(j):
        zero = jnp.zeros((64, 128), F32)
        taps = [[three_v[(i * 3 + t) * 64:(i * 3 + t + 1) * 64, :] for i in range(3)] for t in range(3)]
        w = []
        for g0, g1, g2 in taps:
            w.append((g0, (g0 + g2 + g1) * 0.5, (g0 + g2 - g1) * 0.5, g2)[j])
        for r, (left, right) in enumerate(((w[1], w[0]), (w[2], w[1]), (zero, w[2]), (w[0], zero))):
            for s, part in enumerate((left, right)):
                high, low = halves(part)
                for at, value in ((0, high), (256, high), (512, low)):
                    at = j * 768 + at + r * 64
                    w3[at:at + 64, s * 128:(s + 1) * 128] = value

    def second_weights(i):
        place = [jnp.where(iota((64, 128), 1) == iota((64, 128), 0) + 64 * s, 1.0, 0.0).astype(BF16) for s in range(2)]
        zero = jnp.zeros((32, 64), F32)
        w = [two_v[(i * 3 + j) * 32:(i * 3 + j + 1) * 32, :] for j in range(3)]
        stacks = (jnp.concatenate(w + [zero], axis=0), jnp.concatenate([zero] + w, axis=0))
        for part in range(2):
            value = sum(dot(halves(stack)[part], where) for stack, where in zip(stacks, place)).astype(BF16)
            for r in range(2):
                w2[i * 256 + r * 128:i * 256 + (r + 1) * 128, part * 128:(part + 1) * 128] = value

    def first_weights(i):
        spread = jnp.where(iota((32, 512), 1) % 32 == iota((32, 512), 0), 1.0, 0.0).astype(BF16)
        j, col = iota((32, 512), 0), iota((32, 512), 1)
        g = (j % 16) // 2
        pos = 2 * (col // 128) - 1 + (col % 128) // 32
        for part in range(2):
            value = jnp.zeros((32, 512), F32)
            for s in range(3):
                line = dot(halves(jnp.broadcast_to(one_v[i, s], (16, 32)))[part], spread)[0:1]
                hit = (g - pos + 1 == s) & (pos >= 0) & (pos < 8) & (j % 2 == 0)
                value = value + jnp.where(hit, line, 0.0)
            w1[part * 128 + i * 32:part * 128 + (i + 1) * 32, :] = value.astype(BF16)
            if i == 0:
                w1[part * 128 + 96:part * 128 + 128, :] = jnp.zeros((32, 512), BF16)

    def clear_ends(ref):
        for p in range(4):
            for f in (0, 9):
                ref[p, f] = jnp.zeros((128, 256), BF16)

    def clear_sides(ref):
        for p in (1, 4):
            ref[p, :, :, 128:256] = jnp.zeros((16, 128, 128), BF16)

    def prepare(i):
        if i == 0:
            for load in (2, 3, 4):
                loads[load].wait()
        (
            *[functools.partial(third_weights, t) for t in range(4)],
            *[functools.partial(second_weights, t) for t in range(3)],
            *[functools.partial(first_weights, t) for t in range(3)],
            functools.partial(clear_ends, x1),
            *[functools.partial(clear_sides, ref) for ref in (x2h, x2l)],
        )[i]()

    present = None
    loads[0].wait()
    loads[1].wait()
    for step, *which in ORDER:
        if step == "lengths":
            for name, block in (("b", b_r), ("c1", b_q), ("c3", b_s)):
                wait(("len", name), lens.at[block])
            present = length_lanes()
        else:
            dict(get=get, put=put, permute=permute, tile=tile, post=post, prepare=prepare)[step](*which)
        if (step, *which) == ("get", "xh", 4):
            for name in ("c1", "c3"):
                send(("len", name), lens.at[me_b], lens.at[me_b], far[name])
    ri, ci = iota((128, 128), 0), iota((128, 128), 1)
    where = ri < 0
    for r, (name, places) in enumerate(order.items()):
        for i, (hb, v) in enumerate(places):
            where = where | ((ri == hb * 16 + v) & (ci == r * 32 + unit_of(name, i)))
    sums = cbuf[me_b].reshape(64, 128)
    where = jnp.where(where, 1.0, 0.0).astype(BF16)
    sums = sum(dot(part, where) for part in thirds(sums)) * 0.125
    cbuf[me_b] = sums.reshape(8, 8, 128)
    for name in ("b", "c1", "c3"):
        send(("coarse", name), cbuf.at[me_b], cbuf.at[me_b], (dev | far)[name])

    def column(row):
        return jnp.sum(
            jnp.where(iota((128, 128), 0) == iota((128, 128), 1), row.astype(F32), 0.0), axis=1, keepdims=True
        ).astype(jnp.int32)

    for i in (5, 6, 7):
        loads[i].wait()
    shard, place = column(shard_v[...]), column(local_v[...])
    cy = (shard // 2) % 4
    ca, cb = cy // 2, ((cy + 1) // 2) % 2
    source = (shard // 16) * 4 + ca * 2 + shard % 2
    cross, other = ((shard // 8) % 2) != xh, cb != b
    offset = (place + 2 * ell) % 4
    chb, cv = place // 2, place % 2
    for rule, name in ((cross & ~other, "q"), (other & ~cross, "r"), (cross & other, "s")):
        for i, (hb, v) in enumerate(order[name]):
            hit = rule & (offset == i)
            chb, cv = jnp.where(hit, hb, chb), jnp.where(hit, v, cv)
    cshift = chb * 16 + cv
    cols = iota((128, 96), 1)
    onehot = jnp.where(cols % 32 == source, 1.0, 0.0).astype(BF16)

    for sent in started:
        sent.wait_send()
    messages = pltpu.make_async_remote_copy(
        src_ref=msg.at[pl.ds(0, 31)], dst_ref=rbuf.at[pl.ds(0, 31)], send_sem=msg_send.at[0],
        recv_sem=msg_recv.at[0], device_id=dev["d"], device_id_type=MESH,
    )
    messages.wait_send()
    messages.wait_recv()
    for name, block in (("b", b_r), ("c1", b_q), ("c3", b_s)):
        wait(("coarse", name), cbuf.at[block])
    lane = iota((128, 128), 1)
    kept = (lane < 16) & (lane % 2 == 0)
    near = []
    for f in range(8):
        t = dot(onehot, jnp.concatenate(thirds(rbuf[:, f, :]), axis=0))
        for bit in (64, 32, 16, 1):
            t = jnp.where((cshift // bit) % 2 == 1, pltpu.roll(t, 128 - bit, 1), t)
        there = t > ABSENT / 2
        if f == 0:
            gap = jnp.where(there, 0.0, -3e38)
            for g in range(8):
                pen[g] = gap[:, 2 * g:2 * g + 1]
        t = jnp.where(there & kept, t, 0.0)
        high = t.astype(BF16).astype(F32)
        near.append(high + pltpu.roll(t - high, 16, 1))
    arounds = []
    for f in range(8):
        around = pltpu.roll(near[f], 32, 1)
        if f > 0:
            around = around + near[f - 1]
        if f < 7:
            around = around + pltpu.roll(near[f + 1], 64, 1)
        arounds.append(around.astype(BF16))
    around = jnp.concatenate(arounds, axis=0)
    out = jnp.maximum(dot(jnp.concatenate([around, around], axis=1), w1[...]), 0.0)
    for at, part in zip((0, 128), halves(out)):
        part = part.reshape(8, 128, 512)
        for p in range(4):
            x1[p, 1:9, :, at:at + 128] = part[:, :, p * 128:(p + 1) * 128]

    for p in range(4):
        out = dot(jnp.concatenate([x1[p, i:i + 8].reshape(1024, 256) for i in range(3)], axis=1), w2[...])
        out = jnp.maximum(out[:, :128] + out[:, 128:], 0.0)
        row = [out[f * 128:(f + 1) * 128] for f in range(8)]
        for pair in range(4):
            d1, d2 = row[2 * pair], row[2 * pair + 1]
            mixes = (
                row[2 * pair - 1] - d2 if pair else -d2, d1 + d2, d2 - d1,
                d1 - row[2 * pair + 2] if pair < 3 else d1,
            )
            for j, mix in enumerate(mixes):
                for ref, part in zip((x2h, x2l), halves(mix)):
                    at = j * 4 + pair
                    ref[p + 1, at, :, 0:128] = part
                    ref[p, at, :, 128:192] = part[:, 0:64]
                    ref[p + 2, at, :, 192:256] = part[:, 64:128]

    scale = jnp.concatenate([out_v[...], out_v[...]], axis=1)
    best = [None, None]

    for p in range(4):
        for j in range(4):
            upper = x2h[p + 1, j * 4:j * 4 + 4].reshape(512, 256)
            lower = x2l[p + 1, j * 4:j * 4 + 4].reshape(512, 256)
            products[p % 2, j] = dot(jnp.concatenate([upper, lower, upper], axis=1), w3[j * 768:(j + 1) * 768, :])
        m0, m1, m2, m3 = (products[p % 2, j] for j in range(4))
        for at, out in enumerate((m0 + m1 + m2, m1 - m2 - m3)):
            out = jnp.maximum(out, 0.0) * scale
            for s in range(2):
                total = jnp.sum(out[:, s * 128:(s + 1) * 128], axis=1, keepdims=True)
                total = total.reshape(4, 128, 1) + pen[2 * p + s][None]
                best[at] = total if best[at] is None else jnp.maximum(best[at], total)
    mean = jnp.sum(best[0] + best[1], axis=0) * 0.125
    out_ref[4:5, :] = jnp.sum(
        jnp.where(iota((128, 128), 0) == iota((128, 128), 1), mean, 0.0), axis=0, keepdims=True
    )

    n, col = iota((128, 256), 0), iota((128, 256), 1)
    ny = (n // 2) % 4
    nxh, nb = (n // 8) % 2, ((ny + 1) // 2) % 2
    want = (nxh * 2 + nb) * 64 + (n // 16) * 8 + (ny // 2) * 2 + n % 2
    scores = pick(jnp.where(col == want, 1.0, 0.0).astype(BF16), cbuf[...].reshape(256, 128))
    relation = (nxh != xh).astype(jnp.int32)[:, :128] + 2 * (nb != b).astype(jnp.int32)[:, :128]
    mine = scores
    for r in range(1, 4):
        mine = jnp.where(relation == r, pltpu.roll(scores, 128 - 32 * r, 1), mine)
    out_ref[0:4, :] = mine.T[0:4]


def split_rows(scores_ref, coarse_ref, refined_ref):
    coarse_ref[...] = scores_ref[0:4, :]
    refined_ref[...] = scores_ref[4:5, :]


def local(queries, database, db_frames, cand_shard, cand_local, conv_one, conv_two, conv_three, conv_out):
    anywhere = pl.BlockSpec(memory_space=pltpu.HBM)
    vmem = pl.BlockSpec(memory_space=pltpu.VMEM)
    smem = pl.BlockSpec(memory_space=pltpu.SMEM)
    scores = pl.pallas_call(
        kernel,
        out_shape=jax.ShapeDtypeStruct((8, 128), F32),
        in_specs=[anywhere, anywhere, smem] + [anywhere] * 6,
        out_specs=vmem,
        scratch_shapes=[
            pltpu.VMEM((32, 128, K), BF16),
            pltpu.VMEM((16, 128, K), BF16),
            pltpu.VMEM((4, 2, 256, K), BF16),
            pltpu.VMEM((4, 32, 8, 128), F32),
            pltpu.VMEM((4, 8, 128), F32),
            pltpu.VMEM((32, 8, 128), F32),
            pltpu.VMEM((32, 8, 128), F32),
            pltpu.VMEM((4, 8, 8, 128), F32),
            pltpu.VMEM((256, 256), BF16),
            pltpu.VMEM((1, 128), jnp.int32),
            pltpu.VMEM((1, 128), jnp.int32),
            pltpu.VMEM((3, 3, 1, 32), F32),
            pltpu.VMEM((288, 64), F32),
            pltpu.VMEM((576, 128), F32),
            pltpu.VMEM((1, 128), F32),
            pltpu.VMEM((256, 512), BF16),
            pltpu.VMEM((768, 256), BF16),
            pltpu.VMEM((3072, 256), BF16),
            pltpu.VMEM((4, 10, 128, 256), BF16),
            pltpu.VMEM((6, 16, 128, 256), BF16),
            pltpu.VMEM((6, 16, 128, 256), BF16),
            pltpu.VMEM((2, 4, 512, 256), F32),
            pltpu.VMEM((8, 128, 1), F32),
            pltpu.SemaphoreType.DMA((72,)),
            pltpu.SemaphoreType.DMA((72,)),
            pltpu.SemaphoreType.DMA((1,)),
            pltpu.SemaphoreType.DMA((1,)),
            pltpu.SemaphoreType.DMA((8,)),
        ],
        compiler_params=pltpu.CompilerParams(
            collective_id=0, has_side_effects=True, vmem_limit_bytes=64 * 1024 * 1024
        ),
        cost_estimate=pl.CostEstimate(flops=13_000_000_000, bytes_accessed=2_000_000, transcendentals=0),
    )(
        queries.reshape(128, K), database.reshape(4, 128, K), db_frames, cand_shard.reshape(1, 128),
        cand_local.reshape(1, 128), conv_one, conv_two.reshape(288, 64),
        conv_three.reshape(576, 128), conv_out.reshape(1, 128),
    )
    coarse, refined = pl.pallas_call(
        split_rows,
        out_shape=(jax.ShapeDtypeStruct((4, 128), F32), jax.ShapeDtypeStruct((1, 128), F32)),
    )(scores)
    return coarse.T[None], refined[None]


def solution(mesh):
    in_specs = (
        P("index", "rep", None, None, None),
        P("index", None, None, None),
        P("index"),
        P("index", "rep", None, None),
        P("index", "rep", None),
        P(),
        P(),
        P(),
        P(),
    )
    out_specs = (P("rep", None, "index"), P("index", "rep", None))
    return jax.shard_map(local, mesh=mesh, in_specs=in_specs, out_specs=out_specs, check_vma=False)
```

```python
import functools

import jax
import jax.numpy as jnp
from jax import lax
from jax.experimental import pallas as pl
from jax.experimental.pallas import tpu as pltpu
from jax.sharding import PartitionSpec as P

MESH = pl.DeviceIdType.MESH
F32, BF16 = jnp.float32, jnp.bfloat16
ABSENT = -(2.0 ** 100)
K = 512
ORDER = (
    ("permute", 0), ("permute", 1), ("prepare", 0), ("prepare", 1), ("prepare", 2), ("prepare", 3), ("prepare", 4),
    ("get", "d", (0, 0)), ("prepare", 5), ("prepare", 6), ("prepare", 7), ("prepare", 8), ("prepare", 9),
    ("prepare", 10), ("prepare", 11), ("prepare", 12), ("get", "a", 0), ("put", "+", (1, 2)), ("put", "-", (1, 2)),
    ("get", "+", (1, 1)), ("put", "+", (2, 1)), ("put", "a", 2), ("get", "-", (1, 1)), ("put", "-", (2, 1)),
    ("put", "a", 3), ("get", "a", 1), ("put", "d", (0, 1)), ("get", "+", (1, 0)), ("put", "+", (2, 0)),
    ("put", "d", (1, 0)), ("get", "-", (1, 0)), ("put", "-", (2, 0)), ("put", "d", (2, 0)), ("get", "xh", 0),
    ("put", "xl", 0), ("get", "b", 0), ("put", "xh", 4), ("put", "b", 4), ("put", "xl", 1), ("permute", 2),
    ("get", "d", (0, 1)), ("tile", 0, 0), ("get", "d", (1, 0)), ("get", "d", (2, 0)),
    ("get", "+", (1, 2)), ("put", "+", (2, 2)), ("get", "-", (1, 2)), ("put", "-", (2, 2)), ("get", "xh", 1),
    ("get", "a", 2), ("put", "d", (1, 1)), ("get", "b", 1), ("put", "xh", 5), ("put", "b", 5), ("permute", 3),
    ("tile", 1, 0), ("get", "+", (2, 1)), ("put", "+", (3, 1)), ("put", "a", 4), ("get", "-", (2, 1)),
    ("put", "-", (3, 1)), ("put", "a", 5), ("get", "a", 3), ("put", "d", (2, 1)), ("get", "d", (1, 1)),
    ("tile", 0, 1), ("tile", 1, 1), ("get", "+", (2, 0)), ("put", "+", (3, 0)), ("put", "d", (3, 0)),
    ("get", "-", (2, 0)), ("put", "-", (3, 0)), ("put", "d", (4, 0)), ("get", "d", (2, 1)), ("get", "xl", 0),
    ("tile", 0, 2), ("get", "xh", 4), ("put", "xh", 2), ("get", "b", 4), ("put", "b", 2), ("permute", 4),
    ("get", "d", (3, 0)), ("get", "+", (2, 2)), ("put", "+", (3, 2)), ("get", "-", (2, 2)), ("put", "-", (3, 2)),
    ("get", "d", (4, 0)), ("tile", 1, 2), ("get", "+", (3, 1)), ("put", "+", (4, 1)), ("put", "a", 6),
    ("get", "a", 4), ("put", "d", (3, 1)), ("get", "-", (3, 1)), ("put", "g", 1), ("put", "a", 7), ("get", "xl", 1),
    ("get", "xh", 5), ("get", "b", 5), ("permute", 5), ("permute", 6), ("tile", 2, 2), ("get", "+", (3, 0)),
    ("put", "+", (4, 0)), ("put", "d", (5, 0)), ("get", "a", 5), ("put", "d", (4, 1)), ("get", "d", (3, 1)),
    ("get", "-", (3, 0)), ("put", "g", 0), ("put", "d", (6, 0)), ("tile", 0, 3), ("tile", 1, 3), ("tile", 2, 3),
    ("get", "+", (3, 2)), ("get", "d", (5, 0)), ("get", "-", (3, 2)), ("get", "d", (4, 1)), ("get", "d", (6, 0)),
    ("tile", 0, 4), ("get", "xh", 2), ("get", "b", 2), ("permute", 7), ("get", "a", 6), ("put", "d", (5, 1)),
    ("get", "+", (4, 1)), ("tile", 1, 4), ("tile", 2, 4), ("tile", 3, 4), ("lengths",), ("post", 4), ("get", "g", 1),
    ("get", "d", (5, 1)), ("get", "+", (4, 0)), ("put", "d", (7, 0)), ("tile", 0, 5), ("tile", 1, 5), ("tile", 2, 5),
    ("tile", 3, 5), ("get", "a", 7), ("put", "d", (6, 1)), ("get", "d", (7, 0)), ("get", "g", 0),
    ("put", "d", (7, 1)), ("post", 5), ("tile", 3, 3), ("post", 3), ("tile", 3, 2), ("post", 2), ("get", "d", (6, 1)),
    ("tile", 0, 6), ("get", "d", (7, 1)), ("tile", 0, 7), ("tile", 1, 7), ("tile", 2, 7), ("tile", 3, 7), ("post", 7),
    ("tile", 1, 6), ("tile", 2, 6), ("tile", 3, 6), ("post", 6), ("tile", 2, 1), ("tile", 3, 1), ("post", 1),
    ("tile", 2, 0), ("tile", 3, 0), ("post", 0),
)


def dot(a, b):
    return jnp.dot(a, b, preferred_element_type=F32)


def iota(shape, axis):
    return lax.broadcasted_iota(jnp.int32, shape, axis)


def halves(x):
    high = x.astype(BF16)
    return high, (x - high.astype(F32)).astype(BF16)


def thirds(x):
    high, rest = x.astype(BF16), None
    rest = x - high.astype(F32)
    mid = rest.astype(BF16)
    return high, mid, (rest - mid.astype(F32)).astype(BF16)


def pick(onehot, x):
    y = dot(onehot, jnp.concatenate(thirds(x), axis=1))
    n = x.shape[1]
    return y[:, :n] + (y[:, n:2 * n] + y[:, 2 * n:])


def kernel(
    q_hbm, db_hbm, frames, shard_hbm, local_hbm, one_hbm, two_hbm, three_hbm, out_hbm,
    out_ref,
    qbuf, dbraw, dbp, fmap, lens, msg, rbuf, cbuf, perm,
    shard_v, local_v, one_v, two_v, three_v, out_v,
    w1, w2, w3, x1, x2h, x2l, products, pen,
    send_sem, recv_sem, msg_send, msg_recv, local_sem,
):
    index, rep = lax.axis_index("index"), lax.axis_index("rep")
    c, y, xh, z = index % 2, (index // 2) % 4, (index // 8) % 2, index // 16
    x = xh * 2 + rep
    a, b = y // 2, ((y + 1) // 2) % 2
    ell = rep

    def device(z, x, y, c):
        return (((z * 2 + x // 2) * 4 + y) * 2 + c, x % 2)

    def y_of(a, b):
        return a * 3 + b * (1 - 2 * a)

    me_q = z * 4 + a * 2 + c
    me_b = xh * 2 + b
    b_own, b_q, b_r, b_s = me_b, (1 - xh) * 2 + b, xh * 2 + (1 - b), (1 - xh) * 2 + (1 - b)
    dev = {
        "+": device((z + 1) % 8, x, y, c),
        "-": device((z + 7) % 8, x, y, c),
        "a": device(z, x, 3 - y, c),
        "b": device(z, x, y_of(a, 1 - b), c),
        "d": device(z, x, y, 1 - c),
        "xh": device(z, 3 - x, y, c),
        "xl": device(z, xh * 2 + (1 - rep), y, c),
    }
    far = {
        "c1": device(z, (1 - xh) * 2 + rep, y, c),
        "c3": device(z, (1 - xh) * 2 + rep, y_of(a, 1 - b), c),
    }

    diagonal = device((z + 7) % 8, x, 3 - y, c)

    def row_device(k, da, dc):
        zk, ak, ck = z_at(k), 1 - a if da else a, 1 - c if dc else c
        return zk, ak, ck, device(zk, x, y_of(ak, b), ck)

    barrier = pltpu.get_barrier_semaphore()
    for target in dev.values():
        pl.semaphore_signal(barrier, inc=1, device_id=target, device_id_type=MESH)

    loads = [
        pltpu.make_async_copy(src, dst, local_sem.at[i])
        for i, (src, dst) in enumerate((
            (q_hbm, qbuf.at[me_q]),
            (db_hbm, dbraw.at[pl.ds(me_b * 4, 4)]),
            (three_hbm, three_v),
            (two_hbm, two_v),
            (one_hbm, one_v),
            (shard_hbm, shard_v),
            (local_hbm, local_v),
            (out_hbm, out_v),
        ))
    ]
    for load in loads:
        load.start()

    row8 = iota((8, 128), 0)
    own_lens = jnp.zeros((8, 128), F32)
    for u in range(4):
        own_lens = jnp.where(row8 == u, frames[u].astype(F32), own_lens)
    lens[me_b] = own_lens

    ids, started = {}, []

    def copy(name, src, dst, target):
        sem = ids.setdefault(name, len(ids))
        return pltpu.make_async_remote_copy(
            src_ref=src, dst_ref=dst, send_sem=send_sem.at[sem], recv_sem=recv_sem.at[sem],
            device_id=target, device_id_type=MESH,
        )

    def send(name, src, dst, target):
        started.append(copy(name, src, dst, target))
        started[-1].start()

    def wait(name, dst):
        copy(name, dst, dst, dev["d"]).wait_recv()

    around_z = [(z + ((k + 1) // 2) * (1 - 2 * (k % 2)) + 8) % 8 for k in range(9)]

    def z_at(k):
        return around_z[k]

    def half(zz, aa, h):
        return qbuf.at[zz * 4 + aa * 2 + c, pl.ds(h * 64, 64), :]

    def unit(zz, aa, cc):
        return qbuf.at[zz * 4 + aa * 2 + cc]

    def db_unit(block, u):
        return dbraw.at[block * 4 + u]

    pl.semaphore_wait(barrier, len(dev))

    def ring_send(way, d, item):
        k = 2 * (d - 1) - (1 if way == "+" else 0) if d > 1 else 0
        zz = z_at(k)
        ref = half(zz, 1 - a, 0) if item == 2 else half(zz, a, item)
        src = q_hbm.at[pl.ds(item * 64, 64), :] if d == 1 and item < 2 else ref
        send((way, d, item), src, ref, dev[way])

    def ring_wait(way, d, item):
        zz = z_at(2 * d - (1 if way == "+" else 0))
        wait((way, d, item), half(zz, 1 - a, 0) if item == 2 else half(zz, a, item))

    def db_at(link, position):
        first = {"xh": (2, 3, 1, None, 0, 1), "b": (2, 3, 1, None, 2, 3)}[link]
        block = b_s if position > 3 else b_q if link == "xh" else b_r
        return block, (2 * ell + first[position]) % 4

    def put(link, key):
        name = (link, key)
        if link in "+-":
            ring_send(link, *key)
        elif link == "a":
            if key < 2:
                send(name, q_hbm.at[pl.ds(key * 64, 64), :], half(z, a, key), dev["a"])
            else:
                ref = half(z_at(key - 1), a, 1)
                send(name, ref, ref, dev["a"])
        elif link == "d":
            k, other = key
            ref = unit(z_at(k), 1 - a if other else a, c)
            send(name, ref if k or other else q_hbm, ref, dev["d"])
        elif link == "g":
            ref = half(z_at(6), a, key)
            send(name, ref, ref, diagonal)
        elif link == "xl":
            ref = db_unit(b_r if key else b_q, (2 * ell + 2) % 4)
            send(name, ref, ref, dev["xl"])
        elif key > 3:
            ref = db_unit(b_r if link == "xh" else b_q, (2 * ell + key - 2) % 4)
            send(name, ref, ref, dev[link])
        else:
            first = (0, 1, 3) if link == "xh" else (2, 3, 1)
            u = (2 * ell + first[key]) % 4
            send(name, db_hbm.at[u], db_unit(me_b, u), dev[link])

    def get(link, key):
        name = (link, key)
        if link in "+-":
            ring_wait(link, *key)
        elif link == "a":
            wait(name, half(z, 1 - a, key) if key < 2 else half(z_at(key - 1), 1 - a, 1))
        elif link == "d":
            wait(name, unit(z_at(key[0]), 1 - a if key[1] else a, 1 - c))
        elif link == "g":
            wait(name, half(z_at(7), 1 - a, key))
        elif link == "xl":
            wait(name, db_unit(b_r if key else b_q, 2 * ell))
        else:
            wait(name, db_unit(*db_at(link, key)))

    for link, keys in (
        ("+", ((1, 1),)), ("-", ((1, 1),)), ("a", (0,)), ("+", ((1, 0),)), ("-", ((1, 0),)), ("a", (1,)),
        ("xh", (0,)), ("b", (0,)), ("d", ((0, 0),)), ("xh", (1,)), ("b", (1,)),
    ):
        for key in keys:
            put(link, key)
    send(("len", "b"), lens.at[me_b], lens.at[me_b], dev["b"])

    ri, ci = iota((256, 256), 0), iota((256, 256), 1)
    perm[...] = jnp.where(
        ci == (ri % 2) * 128 + ((ri // 2) % 8) * 16 + ri // 16, 1.0, 0.0
    ).astype(BF16)

    def permute(hb):
        videos = (
            ((b_own, 0), (b_own, 1)), ((b_own, 2), (b_own, 3)),
            (db_at("xh", 0), db_at("b", 0)), (db_at("xh", 1), db_at("b", 1)), (db_at("xh", 4), db_at("b", 4)),
            (db_at("xh", 5), db_at("b", 5)), ((b_q, 2 * ell), (b_r, 2 * ell)), (db_at("xh", 2), db_at("b", 2)),
        )[hb]
        raw = jnp.concatenate([dbraw[block * 4 + u] for block, u in videos], axis=0)
        rows = dot(perm[...], raw).astype(BF16)
        for u in range(16):
            at = (u % 8) * 32 + (hb % 2) * 16
            dbp[hb // 2, u // 8, at:at + 16, :] = rows[u * 16:(u + 1) * 16]

    lane = iota((8, 128), 1)

    def tile(group, k):
        zz = z_at(k)
        left = qbuf[pl.ds(zz * 4, 4)].reshape(512, K)
        top = None
        for t in range(2):
            sim = lax.dot_general(left, dbp[group, t], (((1,), (1,)), ((), ())), preferred_element_type=F32)
            sim = jnp.maximum(sim[:, :128], sim[:, 128:])
            top = sim if top is None else jnp.maximum(top, sim)
        top = jnp.maximum(top, pltpu.roll(top, 64, 1))
        top = jnp.maximum(top, pltpu.roll(top, 32, 1))
        mean = jnp.sum(top.reshape(32, 16, 128), axis=1).reshape(4, 8, 128)
        fmap[group, pl.ds(zz * 4, 4)] = mean

    order = {
        "own": ((0, 0), (0, 1), (1, 0), (1, 1)),
        "q": ((6, 0), (7, 0), (2, 0), (3, 0)),
        "r": ((6, 1), (7, 1), (2, 1), (3, 1)),
        "s": ((4, 0), (5, 0), (4, 1), (5, 1)),
    }
    blocks = {"own": b_own, "q": b_q, "r": b_r, "s": b_s}

    def unit_of(name, i):
        return i if name == "own" else (2 * ell + i) % 4

    def length_lanes():
        total = jnp.zeros((1, 128), F32)
        lane1 = iota((1, 128), 1)
        for name, places in order.items():
            for i, (hb, v) in enumerate(places):
                value = lens[blocks[name], pl.ds(unit_of(name, i), 1), :]
                total = jnp.where((lane1 // 16 == hb) & (lane1 % 2 == v), value, total)
        return (lane1 % 16 // 2).astype(F32) < total

    def post(k):
        zz = z_at(k)
        found = []
        for i in range(4):
            maps = fmap[0, zz * 4 + i]
            for group in range(1, 4):
                maps = jnp.where(lane // 32 == group, fmap[group, zz * 4 + i], maps)
            maps = jnp.where(present, maps * (K ** -0.5 / 16), ABSENT)
            msg[zz * 4 + i] = maps
            found.append(maps)
        for da in (1, 0):
            for dc in (1, 0):
                zk, ak, ck, target = row_device(k, da, dc)
                slot = zk * 4 + ak * 2 + ck
                if k == 0 and da == 0 and dc == 0:
                    rbuf[me_q] = msg[slot]
                else:
                    pltpu.make_async_remote_copy(
                        src_ref=msg.at[slot], dst_ref=rbuf.at[me_q], send_sem=msg_send.at[0],
                        recv_sem=msg_recv.at[0], device_id=target, device_id_type=MESH,
                    ).start()
        rows = jnp.zeros((8, 128), F32)
        for i, maps in enumerate(found):
            for shift in (8, 4, 2):
                maps = jnp.maximum(maps, pltpu.roll(maps, 128 - shift, 1))
            rows = jnp.where(row8 == i, jnp.sum(maps, axis=0, keepdims=True), rows)
        cbuf[me_b, zz] = rows

    def third_weights(j):
        zero = jnp.zeros((64, 128), F32)
        taps = [[three_v[(i * 3 + t) * 64:(i * 3 + t + 1) * 64, :] for i in range(3)] for t in range(3)]
        w = []
        for g0, g1, g2 in taps:
            w.append((g0, (g0 + g2 + g1) * 0.5, (g0 + g2 - g1) * 0.5, g2)[j])
        for r, (left, right) in enumerate(((w[1], w[0]), (w[2], w[1]), (zero, w[2]), (w[0], zero))):
            for s, part in enumerate((left, right)):
                high, low = halves(part)
                for at, value in ((0, high), (256, high), (512, low)):
                    at = j * 768 + at + r * 64
                    w3[at:at + 64, s * 128:(s + 1) * 128] = value

    def second_weights(i):
        place = [jnp.where(iota((64, 128), 1) == iota((64, 128), 0) + 64 * s, 1.0, 0.0).astype(BF16) for s in range(2)]
        zero = jnp.zeros((32, 64), F32)
        w = [two_v[(i * 3 + j) * 32:(i * 3 + j + 1) * 32, :] for j in range(3)]
        stacks = (jnp.concatenate(w + [zero], axis=0), jnp.concatenate([zero] + w, axis=0))
        for part in range(2):
            value = sum(dot(halves(stack)[part], where) for stack, where in zip(stacks, place)).astype(BF16)
            for r in range(2):
                w2[i * 256 + r * 128:i * 256 + (r + 1) * 128, part * 128:(part + 1) * 128] = value

    def first_weights(i):
        spread = jnp.where(iota((32, 512), 1) % 32 == iota((32, 512), 0), 1.0, 0.0).astype(BF16)
        j, col = iota((32, 512), 0), iota((32, 512), 1)
        g = (j % 16) // 2
        pos = 2 * (col // 128) - 1 + (col % 128) // 32
        for part in range(2):
            value = jnp.zeros((32, 512), F32)
            for s in range(3):
                line = dot(halves(jnp.broadcast_to(one_v[i, s], (16, 32)))[part], spread)[0:1]
                hit = (g - pos + 1 == s) & (pos >= 0) & (pos < 8) & (j % 2 == 0)
                value = value + jnp.where(hit, line, 0.0)
            w1[part * 128 + i * 32:part * 128 + (i + 1) * 32, :] = value.astype(BF16)
            if i == 0:
                w1[part * 128 + 96:part * 128 + 128, :] = jnp.zeros((32, 512), BF16)

    def clear_ends(ref):
        for p in range(4):
            for f in (0, 9):
                ref[p, f] = jnp.zeros((128, 256), BF16)

    def clear_sides(ref):
        for p in (1, 4):
            ref[p, :, :, 128:256] = jnp.zeros((16, 128, 128), BF16)

    def prepare(i):
        if i == 0:
            for load in (2, 3, 4):
                loads[load].wait()
        (
            *[functools.partial(third_weights, t) for t in range(4)],
            *[functools.partial(second_weights, t) for t in range(3)],
            *[functools.partial(first_weights, t) for t in range(3)],
            functools.partial(clear_ends, x1),
            *[functools.partial(clear_sides, ref) for ref in (x2h, x2l)],
        )[i]()

    present = None
    loads[0].wait()
    loads[1].wait()
    for step, *which in ORDER:
        if step == "lengths":
            for name, block in (("b", b_r), ("c1", b_q), ("c3", b_s)):
                wait(("len", name), lens.at[block])
            present = length_lanes()
        else:
            dict(get=get, put=put, permute=permute, tile=tile, post=post, prepare=prepare)[step](*which)
        if (step, *which) == ("get", "xh", 4):
            for name in ("c1", "c3"):
                send(("len", name), lens.at[me_b], lens.at[me_b], far[name])
    ri, ci = iota((128, 128), 0), iota((128, 128), 1)
    where = ri < 0
    for r, (name, places) in enumerate(order.items()):
        for i, (hb, v) in enumerate(places):
            where = where | ((ri == hb * 16 + v) & (ci == r * 32 + unit_of(name, i)))
    sums = cbuf[me_b].reshape(64, 128)
    where = jnp.where(where, 1.0, 0.0).astype(BF16)
    sums = sum(dot(part, where) for part in thirds(sums)) * 0.125
    cbuf[me_b] = sums.reshape(8, 8, 128)
    for name in ("b", "c1", "c3"):
        send(("coarse", name), cbuf.at[me_b], cbuf.at[me_b], (dev | far)[name])

    def column(row):
        return jnp.sum(
            jnp.where(iota((128, 128), 0) == iota((128, 128), 1), row.astype(F32), 0.0), axis=1, keepdims=True
        ).astype(jnp.int32)

    for i in (5, 6, 7):
        loads[i].wait()
    shard, place = column(shard_v[...]), column(local_v[...])
    cy = (shard // 2) % 4
    ca, cb = cy // 2, ((cy + 1) // 2) % 2
    source = (shard // 16) * 4 + ca * 2 + shard % 2
    cross, other = ((shard // 8) % 2) != xh, cb != b
    offset = (place + 2 * ell) % 4
    chb, cv = place // 2, place % 2
    for rule, name in ((cross & ~other, "q"), (other & ~cross, "r"), (cross & other, "s")):
        for i, (hb, v) in enumerate(order[name]):
            hit = rule & (offset == i)
            chb, cv = jnp.where(hit, hb, chb), jnp.where(hit, v, cv)
    cshift = chb * 16 + cv
    cols = iota((128, 96), 1)
    onehot = jnp.where(cols % 32 == source, 1.0, 0.0).astype(BF16)

    for sent in started:
        sent.wait_send()
    messages = pltpu.make_async_remote_copy(
        src_ref=msg.at[pl.ds(0, 31)], dst_ref=rbuf.at[pl.ds(0, 31)], send_sem=msg_send.at[0],
        recv_sem=msg_recv.at[0], device_id=dev["d"], device_id_type=MESH,
    )
    messages.wait_send()
    messages.wait_recv()
    for name, block in (("b", b_r), ("c1", b_q), ("c3", b_s)):
        wait(("coarse", name), cbuf.at[block])
    lane = iota((128, 128), 1)
    kept = (lane < 16) & (lane % 2 == 0)
    near = []
    for f in range(8):
        t = dot(onehot, jnp.concatenate(thirds(rbuf[:, f, :]), axis=0))
        for bit in (64, 32, 16, 1):
            t = jnp.where((cshift // bit) % 2 == 1, pltpu.roll(t, 128 - bit, 1), t)
        there = t > ABSENT / 2
        if f == 0:
            gap = jnp.where(there, 0.0, -3e38)
            for g in range(8):
                pen[g] = gap[:, 2 * g:2 * g + 1]
        t = jnp.where(there & kept, t, 0.0)
        high = t.astype(BF16).astype(F32)
        near.append(high + pltpu.roll(t - high, 16, 1))
    arounds = []
    for f in range(8):
        around = pltpu.roll(near[f], 32, 1)
        if f > 0:
            around = around + near[f - 1]
        if f < 7:
            around = around + pltpu.roll(near[f + 1], 64, 1)
        arounds.append(around.astype(BF16))
    around = jnp.concatenate(arounds, axis=0)
    out = jnp.maximum(dot(jnp.concatenate([around, around], axis=1), w1[...]), 0.0)
    for at, part in zip((0, 128), halves(out)):
        part = part.reshape(8, 128, 512)
        for p in range(4):
            x1[p, 1:9, :, at:at + 128] = part[:, :, p * 128:(p + 1) * 128]

    for p in range(4):
        out = dot(jnp.concatenate([x1[p, i:i + 8].reshape(1024, 256) for i in range(3)], axis=1), w2[...])
        out = jnp.maximum(out[:, :128] + out[:, 128:], 0.0)
        row = [out[f * 128:(f + 1) * 128] for f in range(8)]
        for pair in range(4):
            d1, d2 = row[2 * pair], row[2 * pair + 1]
            mixes = (
                row[2 * pair - 1] - d2 if pair else -d2, d1 + d2, d2 - d1,
                d1 - row[2 * pair + 2] if pair < 3 else d1,
            )
            for j, mix in enumerate(mixes):
                for ref, part in zip((x2h, x2l), halves(mix)):
                    at = j * 4 + pair
                    ref[p + 1, at, :, 0:128] = part
                    ref[p, at, :, 128:192] = part[:, 0:64]
                    ref[p + 2, at, :, 192:256] = part[:, 64:128]

    scale = jnp.concatenate([out_v[...], out_v[...]], axis=1)
    best = [None, None]

    for p in range(4):
        for j in range(4):
            upper = x2h[p + 1, j * 4:j * 4 + 4].reshape(512, 256)
            lower = x2l[p + 1, j * 4:j * 4 + 4].reshape(512, 256)
            products[p % 2, j] = dot(jnp.concatenate([upper, lower, upper], axis=1), w3[j * 768:(j + 1) * 768, :])
        m0, m1, m2, m3 = (products[p % 2, j] for j in range(4))
        for at, out in enumerate((m0 + m1 + m2, m1 - m2 - m3)):
            out = jnp.maximum(out, 0.0) * scale
            for s in range(2):
                total = jnp.sum(out[:, s * 128:(s + 1) * 128], axis=1, keepdims=True)
                total = total.reshape(4, 128, 1) + pen[2 * p + s][None]
                best[at] = total if best[at] is None else jnp.maximum(best[at], total)
    mean = jnp.sum(best[0] + best[1], axis=0) * 0.125
    out_ref[4:5, :] = jnp.sum(
        jnp.where(iota((128, 128), 0) == iota((128, 128), 1), mean, 0.0), axis=0, keepdims=True
    )

    n, col = iota((128, 256), 0), iota((128, 256), 1)
    ny = (n // 2) % 4
    nxh, nb = (n // 8) % 2, ((ny + 1) // 2) % 2
    want = (nxh * 2 + nb) * 64 + (n // 16) * 8 + (ny // 2) * 2 + n % 2
    scores = pick(jnp.where(col == want, 1.0, 0.0).astype(BF16), cbuf[...].reshape(256, 128))
    relation = (nxh != xh).astype(jnp.int32)[:, :128] + 2 * (nb != b).astype(jnp.int32)[:, :128]
    mine = scores
    for r in range(1, 4):
        mine = jnp.where(relation == r, pltpu.roll(scores, 128 - 32 * r, 1), mine)
    out_ref[0:4, :] = mine.T[0:4]


def split_rows(scores_ref, coarse_ref, refined_ref):
    coarse_ref[...] = scores_ref[0:4, :]
    refined_ref[...] = scores_ref[4:5, :]


def local(queries, database, db_frames, cand_shard, cand_local, conv_one, conv_two, conv_three, conv_out):
    anywhere = pl.BlockSpec(memory_space=pltpu.HBM)
    vmem = pl.BlockSpec(memory_space=pltpu.VMEM)
    smem = pl.BlockSpec(memory_space=pltpu.SMEM)
    scores = pl.pallas_call(
        kernel,
        out_shape=jax.ShapeDtypeStruct((8, 128), F32),
        in_specs=[anywhere, anywhere, smem] + [anywhere] * 6,
        out_specs=vmem,
        scratch_shapes=[
            pltpu.VMEM((32, 128, K), BF16),
            pltpu.VMEM((16, 128, K), BF16),
            pltpu.VMEM((4, 2, 256, K), BF16),
            pltpu.VMEM((4, 32, 8, 128), F32),
            pltpu.VMEM((4, 8, 128), F32),
            pltpu.VMEM((32, 8, 128), F32),
            pltpu.VMEM((32, 8, 128), F32),
            pltpu.VMEM((4, 8, 8, 128), F32),
            pltpu.VMEM((256, 256), BF16),
            pltpu.VMEM((1, 128), jnp.int32),
            pltpu.VMEM((1, 128), jnp.int32),
            pltpu.VMEM((3, 3, 1, 32), F32),
            pltpu.VMEM((288, 64), F32),
            pltpu.VMEM((576, 128), F32),
            pltpu.VMEM((1, 128), F32),
            pltpu.VMEM((256, 512), BF16),
            pltpu.VMEM((768, 256), BF16),
            pltpu.VMEM((3072, 256), BF16),
            pltpu.VMEM((4, 10, 128, 256), BF16),
            pltpu.VMEM((6, 16, 128, 256), BF16),
            pltpu.VMEM((6, 16, 128, 256), BF16),
            pltpu.VMEM((2, 4, 512, 256), F32),
            pltpu.VMEM((8, 128, 1), F32),
            pltpu.SemaphoreType.DMA((72,)),
            pltpu.SemaphoreType.DMA((72,)),
            pltpu.SemaphoreType.DMA((1,)),
            pltpu.SemaphoreType.DMA((1,)),
            pltpu.SemaphoreType.DMA((8,)),
        ],
        compiler_params=pltpu.CompilerParams(
            collective_id=0, has_side_effects=True, vmem_limit_bytes=64 * 1024 * 1024
        ),
        cost_estimate=pl.CostEstimate(flops=13_000_000_000, bytes_accessed=2_000_000, transcendentals=0),
    )(
        queries.reshape(128, K), database.reshape(4, 128, K), db_frames, cand_shard.reshape(1, 128),
        cand_local.reshape(1, 128), conv_one, conv_two.reshape(288, 64),
        conv_three.reshape(576, 128), conv_out.reshape(1, 128),
    )
    coarse, refined = pl.pallas_call(
        split_rows,
        out_shape=(jax.ShapeDtypeStruct((4, 128), F32), jax.ShapeDtypeStruct((1, 128), F32)),
    )(scores)
    return coarse.T[None], refined[None]


def solution(mesh):
    in_specs = (
        P("index", "rep", None, None, None),
        P("index", None, None, None),
        P("index"),
        P("index", "rep", None, None),
        P("index", "rep", None),
        P(),
        P(),
        P(),
        P(),
    )
    out_specs = (P("rep", None, "index"), P("index", "rep", None))
    return jax.shard_map(local, mesh=mesh, in_specs=in_specs, out_specs=out_specs, check_vma=False)
```
